128 devices in a mesh: row: 4 (over x_lo, core), col: 32 (over z, y, x_hi).
Axes of the slice: x: 4 (x_hi: 2, x_lo: 2; x = x_hi * 2 + x_lo), y: 4, z: 4, core: 2. Of those that a mesh axis runs over, the one named last changes fastest.
Arguments:
- matrix: float32 [16384, 16384], P('row', 'col'), as said below
- right_sides: float32 [16384, 256], P('row'), may hold values from -6 to 6
Outputs:
- factored: float32 [16384, 16384], P('row', 'col')
- solved: float32 [16384, 256], P('row')
The draws below stay inside these ranges and needn't reach their ends.
Inputs may be any that keep to these rules, and one draw needn't show every extreme that they name: `matrix`: symmetric and positive definite in natural order.
All inputs are finite; a program needn't handle non-finite values.
Results may differ from the reference program's by a relative error of at most 0.0001.
Values sent between devices are 32-bit elements; how exact they have to be, the bound alone decides.
No kernel may reach another device: no remote copies, remote signals or barrier semaphores. Data moves between devices by JAX's collectives and lax.ppermute only.
A program may use at most 192 MiB of HBM per device.

```python
import math
import jax
import jax.numpy as jnp
from jax import lax

NB = 512
PANELS = 2
RHS = 256
ORDER = 16384
ROW_BLOCKS = 8


def draw_matrix(key, part):
    key = jax.random.fold_in(key, 11)
    noise_key = jax.random.fold_in(key, 0)
    diag_key = jax.random.fold_in(key, 1)
    weight_key = jax.random.fold_in(key, 3)
    coupling = jax.random.uniform(noise_key, (ORDER, ORDER), jnp.float32, -1.0, 1.0)
    coupling = 0.5 * (coupling + coupling.T)
    diagonal = jax.random.uniform(diag_key, (ORDER,), jnp.float32, 1.6, 3.2) * math.sqrt(ORDER)
    positions = jnp.arange(ORDER, dtype=jnp.int32)
    whole = jnp.where(positions[:, None] == positions[None, :], diagonal[:, None], coupling)
    facet_weights = jax.random.uniform(weight_key, (ORDER,), jnp.float32, 0.5, 1.5)
    distance = jnp.abs(positions[:, None] - positions[None, :]).astype(jnp.float32)
    kernel = jnp.exp(-distance / (0.5 * NB))
    whole = whole + 0.6 * math.sqrt(ORDER) * facet_weights[:, None] * facet_weights[None, :] * kernel
    row_groups = ORDER // (NB * ROW_BLOCKS)
    shaped = whole.reshape(ROW_BLOCKS, row_groups, NB, ORDER)
    return shaped.transpose(1, 0, 2, 3).reshape(ORDER, ORDER)


def block_scale(rng, shape, shards, least, top_value):
    factor_of = 1.0
    for position, blocks in shards:
        heights = jax.random.uniform(jax.random.fold_in(jax.random.fold_in(rng, 6), position), (blocks,), jnp.float32, least / len(shards), top_value / len(shards))
        factor_of = factor_of * jnp.repeat(jnp.exp(heights), shape[position] // blocks).reshape((-1,) + (1,) * (len(shape) - 1 - position))
    return factor_of


def scatter_about(rng, dims, spread, limit, cuts=(), held_as=jnp.bfloat16):
    level = block_scale(rng, dims, cuts, -0.22, 0.18) if cuts else 1.0
    drawn = jax.random.normal(rng, dims, jnp.float32) * spread * level
    return jnp.minimum(jnp.maximum(drawn, -limit), limit).astype(held_as)


def setup_inputs(seed: int = 0) -> dict:
    key_of = jax.random.split(jax.random.key(seed), 3)
    return {
        "matrix": draw_matrix(jax.random.fold_in(key_of[2], 71), 0),
        "right_sides": scatter_about(key_of[1], (ORDER, RHS), 1.0, 6.0, ((0, 4),), jnp.float32),
    }


def to_global(stored):
    row_groups = ORDER // (NB * ROW_BLOCKS)
    shaped = stored.reshape(row_groups, ROW_BLOCKS, NB, stored.shape[1])
    return shaped.transpose(1, 0, 2, 3).reshape(stored.shape)

def to_stored(whole):
    row_groups = ORDER // (NB * ROW_BLOCKS)
    shaped = whole.reshape(ROW_BLOCKS, row_groups, NB, whole.shape[1])
    return shaped.transpose(1, 0, 2, 3).reshape(whole.shape)

def reference(matrix, right_sides):
    work = to_global(matrix)
    rhs = to_global(right_sides)
    factors = []
    panels = []
    for current in range(PANELS):
        row_start = current * NB
        row_end = row_start + NB
        factor = jnp.linalg.cholesky(work[row_start:row_end, row_start:row_end])
        beneath = jax.scipy.linalg.solve_triangular(factor, work[row_end:, row_start:row_end].T, lower=True).T
        column = jnp.concatenate([jnp.zeros((row_start, NB), jnp.float32), factor, beneath], axis=0)
        work = work.at[:, row_start:row_end].set(column)
        product = jnp.dot(beneath, beneath.T, precision=lax.Precision.HIGHEST)
        work = work.at[row_end:, row_end:].add(-product)
        factors.append(factor)
        panels.append(beneath)
    edge = PANELS * NB
    work = work.at[:edge, edge:].set(jnp.float32(0.0))
    for current in range(PANELS):
        row_start = current * NB
        row_end = row_start + NB
        answer = jax.scipy.linalg.solve_triangular(factors[current], rhs[row_start:row_end], lower=True)
        rhs = rhs.at[row_start:row_end].set(answer)
        rhs = rhs.at[row_end:].add(-jnp.dot(panels[current], answer, precision=lax.Precision.HIGHEST))
    return (to_stored(work), to_stored(rhs))
```

```python
import functools
import jax
import jax.numpy as jnp
from jax import lax
from jax.experimental import pallas as pl
from jax.experimental.pallas import tpu as pltpu
from jax.sharding import PartitionSpec as P

NB = 512
EDGE = 1024
TILE = 128
AXES = ("row", "col")
F32 = jnp.float32
BF16 = jnp.bfloat16
NN = (((1,), (0,)), ((), ()))
NT = (((1,), (1,)), ((), ()))
VMEM = pl.BlockSpec(memory_space=pltpu.VMEM)


def device_index(x, y, z, core):
    return ((x % 2) * 2 + core) * 32 + (z % 4) * 8 + (y % 4) * 2 + (x % 4) // 2


def route(rule):
    pairs = []
    for x in range(4):
        for y in range(4):
            for z in range(4):
                for core in range(2):
                    target = rule(x, y, z, core)
                    if target is not None:
                        pairs.append((device_index(x, y, z, core), device_index(*target)))
    return pairs


def send(value, rule):
    return lax.ppermute(value, AXES, route(rule))


def swap_cores(value):
    return send(value, lambda x, y, z, c: (x, y, z, 1 - c))


def split(value):
    high = value.astype(BF16)
    return high, (value - high.astype(F32)).astype(BF16)


def dot3(a, b, dims=NN):
    ah, al = split(a)
    bh, bl = split(b)
    mul = lambda p, q: lax.dot_general(p, q, dims, preferred_element_type=F32)
    return mul(ah, bh) + (mul(ah, bl) + mul(al, bh))


def dot_full(a, b, dims=NN):
    return lax.dot_general(a, b, dims, precision=lax.Precision.HIGHEST, preferred_element_type=F32)


def factor_tile(work, inverse, factor_t):
    rows = lax.broadcasted_iota(jnp.int32, (TILE, TILE), 0)
    lanes = lax.broadcasted_iota(jnp.int32, (TILE, TILE), 1)
    inverse[...] = jnp.where(rows == lanes, F32(1), F32(0))
    lane8 = lax.broadcasted_iota(jnp.int32, (8, TILE), 1)

    def group(g, carry):
        top = work[0:8, :]
        cols = [jnp.broadcast_to(top[:, s : s + 1], (8, TILE)) for s in range(8)]
        e = [[cols[s][t : t + 1, :] if s <= t else None for s in range(8)] for t in range(8)]
        low = [[None] * 8 for _ in range(8)]
        scale = [None] * 8
        for s in range(8):
            r = lax.rsqrt(e[s][s])
            r = r * (F32(1.5) - F32(0.5) * e[s][s] * r * r)
            scale[s] = r
            for t in range(s + 1, 8):
                low[t][s] = e[t][s] * r
            for u in range(s + 1, 8):
                for t in range(u, 8):
                    e[t][u] = e[t][u] - low[t][s] * low[u][s]
        inv = [[None] * 8 for _ in range(8)]
        for s in range(8):
            inv[s][s] = scale[s]
            for t in range(s + 1, 8):
                total = low[t][s] * inv[s][s]
                for u in range(s + 1, t):
                    total = total + low[t][u] * inv[u][s]
                inv[t][s] = -total * scale[t]
        zero = jnp.zeros((1, TILE), F32)
        eye = inverse[pl.ds(pl.multiple_of(g * 8, 8), 8), :]
        upper = None
        solved = None
        for t in range(8):
            column = jnp.concatenate([inv[s][t] if s >= t else zero for s in range(8)], axis=0)
            a = column * top[t : t + 1, :]
            b = column * eye[t : t + 1, :]
            upper = a if upper is None else upper + a
            solved = b if solved is None else solved + b
        upper = jnp.where(lane8 < TILE - 8 * g, upper, F32(0))
        factor_t[pl.ds(pl.multiple_of(g * 8, 8), 8), :] = pltpu.roll(upper, 8 * g, 1)
        side = upper.T
        for q in range(1, 16):
            at = pl.ds(pl.multiple_of(((g + q) % 16) * 8, 8), 8)
            new = work[8 * q : 8 * q + 8, :]
            row = inverse[at, :]
            for s in range(8):
                mult = jnp.broadcast_to(side[8 * q : 8 * q + 8, s : s + 1], (8, TILE))
                new = new - mult * upper[s : s + 1, :]
                row = row - mult * solved[s : s + 1, :]
            work[8 * q - 8 : 8 * q, :] = pltpu.roll(new, TILE - 8, 1)
            inverse[at, :] = row
        inverse[pl.ds(pl.multiple_of(g * 8, 8), 8), :] = solved
        return carry

    lax.fori_loop(0, 16, group, 0)


def factor_kernel(a00, a10, a11, low, inv, inv_t, mat, work, tile_inv, tile_t):
    rows = lax.broadcasted_iota(jnp.int32, (TILE, TILE), 0)
    lanes = lax.broadcasted_iota(jnp.int32, (TILE, TILE), 1)
    mat[0:NB, 0:NB] = a00[...]
    mat[NB:EDGE, 0:NB] = a10[...]
    mat[NB:EDGE, NB:EDGE] = a11[...]
    low[...] = jnp.zeros_like(low)
    inv[...] = jnp.zeros_like(inv)
    inv_t[...] = jnp.zeros_like(inv_t)
    for b in range(EDGE // TILE):
        s, e = b * TILE, (b + 1) * TILE
        work[...] = mat[s:e, s:e]
        factor_tile(work, tile_inv, tile_t)
        x = jnp.where(rows >= lanes, tile_inv[...], F32(0))
        low[s:e, s:e] = jnp.where(rows >= lanes, tile_t[...].T, F32(0))
        inv[s:e, s:e] = x
        inv_t[s:e, s:e] = x.T
        if b > 0:
            left = dot_full(low[s:e, 0:s], inv[0:s, 0:s])
            left = -dot_full(x, left)
            inv[s:e, 0:s] = left
            inv_t[0:s, s:e] = left.T
        if e < EDGE:
            panel = dot_full(mat[e:EDGE, s:e], x, NT)
            low[e:EDGE, s:e] = panel
            for c in range(e, EDGE, 2 * TILE):
                d = min(c + 2 * TILE, EDGE)
                mat[c:EDGE, c:d] = mat[c:EDGE, c:d] - dot_full(panel[c - e :], panel[c - e : d - e], NT)


def solve_kernel(col_ref, g0, g1, inv, inv_t, wh, wl, y, mid):
    col = col_ref[0]
    step = 256
    for b in range(EDGE // step):
        s, e = b * step, (b + 1) * step
        if e <= NB:
            part = dot3(inv[s:e, 0:e], g0[0:e, :])
        else:
            part = dot3(inv[s:e, 0:NB], g0[...]) + dot3(inv[s:e, NB:e], g1[0 : e - NB, :])
        y[s:e, :] = part[:, NB:]
        mid[s:e, NB:] = part[:, NB:]
        rows = lax.broadcasted_iota(jnp.int32, (step, NB), 0) + s
        lanes = lax.broadcasted_iota(jnp.int32, (step, NB), 1) + col * NB
        mid[s:e, 0:NB] = jnp.where(col < 2, jnp.where(rows == lanes, F32(-1), F32(0)), part[:, 0:NB])
    for b in range(EDGE // step):
        s, e = b * step, (b + 1) * step
        h, l = split(dot3(inv_t[s:e, s:EDGE], mid[s:EDGE, :]))
        wh[s:e, :] = h
        wl[s:e, :] = l


def update_kernel(place, rows_ref, wh, wl, mat, rhs, special, y, out, out_rhs):
    step = pl.program_id(0)
    row, col = place[0], place[1]
    rh, rl = split(rows_ref[...])
    mul = lambda p, q: lax.dot_general(p, q, NN, preferred_element_type=F32)
    acc = mul(rh, wh[...]) + (mul(rh, wl[...]) + mul(rl, wh[...]))
    base = jnp.where(col < 2, F32(0), mat[...])
    out[...] = base - acc[:, 0:NB]
    out_rhs[...] = rhs[...] - acc[:, NB:]

    @pl.when(jnp.logical_and(step == 0, row < 2))
    def _():
        out[...] = special[...]
        out_rhs[...] = y[...]


def ordered(parts, first):
    both = jnp.concatenate(parts + parts, axis=0)
    size = parts[0].shape[0]
    return lax.dynamic_slice_in_dim(both, (4 - first) % 4 * size, 4 * size, 0)


def spread_leading(block, z, y):
    at_origin = lambda f: (lambda X, Y, Z, C: f(X, Y, Z, C) if (X, Y, Z) == (0, 0, 0) else None)
    part = block.shape[0] // 4
    got = jnp.where(z == 0, block[0:part], F32(0))
    for d in (1, 2, 3):
        got = got + send(block[d * part : (d + 1) * part], at_origin(lambda X, Y, Z, C, d=d: (0, 0, d, C)))
    small = part // 4
    mine = jnp.where(y == 0, got[0:small], F32(0))
    for d in (1, 2, 3):
        mine = mine + send(
            got[d * small : (d + 1) * small], lambda X, Y, Z, C, d=d: (0, d, Z, C) if (X, Y) == (0, 0) else None
        )
    x = lax.axis_index("col") % 2 * 2 + lax.axis_index("row") // 2
    all_x = jnp.where(x == 0, mine, F32(0))
    for d in (1, 2, 3):
        all_x = all_x + send(mine, lambda X, Y, Z, C, d=d: (d, Y, Z, C) if X == 0 else None)
    ring_y = ordered([all_x] + [send(all_x, lambda X, Y, Z, C, d=d: (X, Y - d, Z, C)) for d in (1, 2, 3)], y)
    return ordered([ring_y] + [send(ring_y, lambda X, Y, Z, C, d=d: (X, Y, Z - d, C)) for d in (1, 2, 3)], z)


def body(matrix, right_sides):
    row = lax.axis_index("row")
    col = lax.axis_index("col")
    core, x_lo = row % 2, row // 2
    z, y = col // 8, col // 2 % 4
    first = matrix[0:NB]

    corner = send(first, lambda X, Y, Z, C: (0, 0, 0, 0) if (X, Y, Z, C) == (2, 0, 0, 1) else None)
    corner2 = swap_cores(corner[NB // 2 :])
    extra = jnp.where(core == 0, corner[0 : NB // 2], corner2)
    leading = spread_leading(jnp.concatenate([first, extra], axis=0), z, y)
    other = swap_cores(leading)
    lead0 = jnp.where(core == 0, leading, other)
    lead1 = jnp.where(core == 0, other, leading)
    a00, a10 = lead0[0:NB], lead1[0:NB]
    a11 = jnp.concatenate([lead0[NB:], lead1[NB:]], axis=0)

    top = jnp.concatenate([first, right_sides[0:NB]], axis=1)
    crossed = send(top, lambda X, Y, Z, C: (X + 1, Y, Z, C) if X % 2 == 0 else None)
    own = jnp.where(x_lo == 0, top, crossed)
    partner = swap_cores(own)
    g0 = jnp.where(core == 0, own, partner)
    g1 = jnp.where(core == 0, partner, own)

    rows_t = jnp.concatenate([g0[:, 0:NB].T, g1[:, 0:NB].T], axis=1)
    quarter = lambda t: lax.dynamic_slice_in_dim(rows_t, t * TILE, TILE, 0)
    piece = jnp.where(col % 4 == row, quarter(row), F32(0))
    for s in (1, 2, 3):

        def rule(X, Y, Z, C, s=s):
            r = (X % 2) * 2 + C
            t = (Y % 2) * 2 + X // 2
            if t != r:
                return None
            t = r ^ s
            return (X % 2 + 2 * (t % 2), Y // 2 * 2 + t // 2, Z, C)

        piece = piece + send(quarter(jnp.bitwise_xor(row, s)), rule)
    panel_rows = lax.all_gather(piece, "col", axis=0, tiled=True)

    square = jax.ShapeDtypeStruct((EDGE, EDGE), F32)
    low, inv, inv_t = pl.pallas_call(
        factor_kernel,
        out_shape=(square, square, square),
        in_specs=[VMEM] * 3,
        out_specs=(VMEM,) * 3,
        scratch_shapes=[
            pltpu.VMEM((EDGE, EDGE), F32),
            pltpu.VMEM((TILE, TILE), F32),
            pltpu.VMEM((TILE, TILE), F32),
            pltpu.VMEM((TILE, TILE), F32),
        ],
        compiler_params=pltpu.CompilerParams(vmem_limit_bytes=48 << 20),
        cost_estimate=pl.CostEstimate(flops=100_000_000_000, bytes_accessed=16 << 20, transcendentals=0),
        name="factor",
    )(a00, a10, a11)

    width = NB + right_sides.shape[1]
    wh, wl, answer = pl.pallas_call(
        solve_kernel,
        out_shape=(
            jax.ShapeDtypeStruct((EDGE, width), BF16),
            jax.ShapeDtypeStruct((EDGE, width), BF16),
            jax.ShapeDtypeStruct((EDGE, width - NB), F32),
        ),
        in_specs=[pl.BlockSpec(memory_space=pltpu.SMEM)] + [VMEM] * 4,
        out_specs=(VMEM,) * 3,
        scratch_shapes=[pltpu.VMEM((EDGE, width), F32)],
        compiler_params=pltpu.CompilerParams(vmem_limit_bytes=48 << 20),
        cost_estimate=pl.CostEstimate(flops=10_000_000_000, bytes_accessed=16 << 20, transcendentals=0),
        name="solve",
    )(col.reshape(1), g0, g1, inv, inv_t)

    at = row % 2 * NB
    lower = lax.dynamic_slice(low, (at, col % 2 * NB), (NB, NB))
    special = jnp.where(col < 2, lower, F32(0))
    answer = lax.dynamic_slice_in_dim(answer, at, NB, 0)

    blocks = matrix.shape[0] // NB
    grid_spec = pltpu.PrefetchScalarGridSpec(
        num_scalar_prefetch=1,
        grid=(blocks,),
        in_specs=[
            pl.BlockSpec((NB, EDGE), lambda i, place: (i, 0)),
            pl.BlockSpec((EDGE, width), lambda i, place: (0, 0)),
            pl.BlockSpec((EDGE, width), lambda i, place: (0, 0)),
            pl.BlockSpec((NB, NB), lambda i, place: (i, 0)),
            pl.BlockSpec((NB, width - NB), lambda i, place: (i, 0)),
            pl.BlockSpec((NB, NB), lambda i, place: (0, 0)),
            pl.BlockSpec((NB, width - NB), lambda i, place: (0, 0)),
        ],
        out_specs=[
            pl.BlockSpec((NB, NB), lambda i, place: (i, 0)),
            pl.BlockSpec((NB, width - NB), lambda i, place: (i, 0)),
        ],
    )
    return pl.pallas_call(
        update_kernel,
        grid_spec=grid_spec,
        out_shape=(
            jax.ShapeDtypeStruct(matrix.shape, F32),
            jax.ShapeDtypeStruct(right_sides.shape, F32),
        ),
        compiler_params=pltpu.CompilerParams(vmem_limit_bytes=56 << 20),
        cost_estimate=pl.CostEstimate(flops=20_000_000_000, bytes_accessed=44 << 20, transcendentals=0),
        name="update",
    )(jnp.stack([row, col]), panel_rows, wh, wl, matrix, right_sides, special, answer)


def solution(mesh):
    specs = (P("row", "col"), P("row", None))
    return jax.shard_map(body, mesh=mesh, in_specs=specs, out_specs=specs, check_vma=False)
```

```python
import functools
import jax
import jax.numpy as jnp
from jax import lax
from jax.experimental import pallas as pl
from jax.experimental.pallas import tpu as pltpu
from jax.sharding import PartitionSpec as P

NB = 512
EDGE = 1024
TILE = 128
AXES = ("row", "col")
F32 = jnp.float32
BF16 = jnp.bfloat16
NN = (((1,), (0,)), ((), ()))
NT = (((1,), (1,)), ((), ()))
VMEM = pl.BlockSpec(memory_space=pltpu.VMEM)


def device_index(x, y, z, core):
    return ((x % 2) * 2 + core) * 32 + (z % 4) * 8 + (y % 4) * 2 + (x % 4) // 2


def route(rule):
    pairs = []
    for x in range(4):
        for y in range(4):
            for z in range(4):
                for core in range(2):
                    target = rule(x, y, z, core)
                    if target is not None:
                        pairs.append((device_index(x, y, z, core), device_index(*target)))
    return pairs


def send(value, rule):
    return lax.ppermute(value, AXES, route(rule))


def swap_cores(value):
    return send(value, lambda x, y, z, c: (x, y, z, 1 - c))


def split(value):
    high = value.astype(BF16)
    return high, (value - high.astype(F32)).astype(BF16)


def dot3(a, b, dims=NN):
    ah, al = split(a)
    bh, bl = split(b)
    mul = lambda p, q: lax.dot_general(p, q, dims, preferred_element_type=F32)
    return mul(ah, bh) + (mul(ah, bl) + mul(al, bh))


def dot_full(a, b, dims=NN):
    return lax.dot_general(a, b, dims, precision=lax.Precision.HIGHEST, preferred_element_type=F32)


def factor_tile(work, inverse, factor_t):
    rows = lax.broadcasted_iota(jnp.int32, (TILE, TILE), 0)
    lanes = lax.broadcasted_iota(jnp.int32, (TILE, TILE), 1)
    inverse[...] = jnp.where(rows == lanes, F32(1), F32(0))
    lane8 = lax.broadcasted_iota(jnp.int32, (8, TILE), 1)

    def group(g, carry):
        top = work[0:8, :]
        cols = [jnp.broadcast_to(top[:, s : s + 1], (8, TILE)) for s in range(8)]
        e = [[cols[s][t : t + 1, :] if s <= t else None for s in range(8)] for t in range(8)]
        low = [[None] * 8 for _ in range(8)]
        scale = [None] * 8
        for s in range(8):
            r = lax.rsqrt(e[s][s])
            r = r * (F32(1.5) - F32(0.5) * e[s][s] * r * r)
            scale[s] = r
            for t in range(s + 1, 8):
                low[t][s] = e[t][s] * r
            for u in range(s + 1, 8):
                for t in range(u, 8):
                    e[t][u] = e[t][u] - low[t][s] * low[u][s]
        inv = [[None] * 8 for _ in range(8)]
        for s in range(8):
            inv[s][s] = scale[s]
            for t in range(s + 1, 8):
                total = low[t][s] * inv[s][s]
                for u in range(s + 1, t):
                    total = total + low[t][u] * inv[u][s]
                inv[t][s] = -total * scale[t]
        zero = jnp.zeros((1, TILE), F32)
        eye = inverse[pl.ds(pl.multiple_of(g * 8, 8), 8), :]
        upper = None
        solved = None
        for t in range(8):
            column = jnp.concatenate([inv[s][t] if s >= t else zero for s in range(8)], axis=0)
            a = column * top[t : t + 1, :]
            b = column * eye[t : t + 1, :]
            upper = a if upper is None else upper + a
            solved = b if solved is None else solved + b
        upper = jnp.where(lane8 < TILE - 8 * g, upper, F32(0))
        factor_t[pl.ds(pl.multiple_of(g * 8, 8), 8), :] = pltpu.roll(upper, 8 * g, 1)
        side = upper.T
        for q in range(1, 16):
            at = pl.ds(pl.multiple_of(((g + q) % 16) * 8, 8), 8)
            new = work[8 * q : 8 * q + 8, :]
            row = inverse[at, :]
            for s in range(8):
                mult = jnp.broadcast_to(side[8 * q : 8 * q + 8, s : s + 1], (8, TILE))
                new = new - mult * upper[s : s + 1, :]
                row = row - mult * solved[s : s + 1, :]
            work[8 * q - 8 : 8 * q, :] = pltpu.roll(new, TILE - 8, 1)
            inverse[at, :] = row
        inverse[pl.ds(pl.multiple_of(g * 8, 8), 8), :] = solved
        return carry

    lax.fori_loop(0, 16, group, 0)


def factor_blocks(blocks, mat, low, inv, inv_t, work, tile_inv, tile_t):
    rows = lax.broadcasted_iota(jnp.int32, (TILE, TILE), 0)
    lanes = lax.broadcasted_iota(jnp.int32, (TILE, TILE), 1)
    for b in blocks:
        s, e = b * TILE, (b + 1) * TILE
        work[...] = mat[s:e, s:e]
        factor_tile(work, tile_inv, tile_t)
        x = jnp.where(rows >= lanes, tile_inv[...], F32(0))
        low[s:e, s:e] = jnp.where(rows >= lanes, tile_t[...].T, F32(0))
        inv[s:e, s:e] = x
        inv_t[s:e, s:e] = x.T
        if b > 0:
            left = dot_full(low[s:e, 0:s], inv[0:s, 0:s])
            left = -dot_full(x, left)
            inv[s:e, 0:s] = left
            inv_t[0:s, s:e] = left.T
        if e < NB:
            panel = dot_full(mat[e:NB, s:e], x, NT)
            low[e:NB, s:e] = panel
            for c in range(e, NB, 2 * TILE):
                d = min(c + 2 * TILE, NB)
                mat[c:NB, c:d] = mat[c:NB, c:d] - dot_full(panel[c - e :], panel[c - e : d - e], NT)


def open_kernel(source, mat, low, inv, inv_t, work, tile_inv, tile_t):
    mat[...] = source[...]
    low[...] = jnp.zeros_like(low)
    inv[...] = jnp.zeros_like(inv)
    inv_t[...] = jnp.zeros_like(inv_t)
    factor_blocks((0, 1), mat, low, inv, inv_t, work, tile_inv, tile_t)


def carry_on(sources, mat, low, inv, inv_t, tiles):
    for source, target in zip(sources, (mat, low, inv, inv_t)):
        target[...] = source[...]
    factor_blocks((2, 3), mat, low, inv, inv_t, *tiles)


def close_kernel(m, l, i, t, low, inv, inv_t, mat, *tiles):
    carry_on((m, l, i, t), mat, low, inv, inv_t, tiles)


def below_kernel(m, l, i, t, a10, a11, low, inv, inv_t, below, below_t, rest, mat, *tiles):
    carry_on((m, l, i, t), mat, low, inv, inv_t, tiles)
    panel = dot_full(a10[...], inv_t[...])
    below[...] = panel
    below_t[...] = panel.T
    rest[...] = a11[...] - dot_full(panel, panel, NT)


def squares(kernel, name, outs, held, *args):
    return pl.pallas_call(
        kernel,
        out_shape=(jax.ShapeDtypeStruct((NB, NB), F32),) * outs,
        in_specs=[VMEM] * len(args),
        out_specs=(VMEM,) * outs,
        scratch_shapes=[pltpu.VMEM((NB, NB), F32)] * held + [pltpu.VMEM((TILE, TILE), F32)] * 3,
        compiler_params=pltpu.CompilerParams(vmem_limit_bytes=24 << 20),
        cost_estimate=pl.CostEstimate(flops=30_000_000_000, bytes_accessed=len(args) << 20, transcendentals=0),
        name=name,
    )(*args)


def factor_all(a00, a10, a11):
    state = squares(open_kernel, "open", 4, 0, a00)
    l0, x0, _, l10, _, rest = squares(below_kernel, "below", 6, 1, *state, a10, a11)
    state = squares(open_kernel, "open", 4, 0, rest)
    l1, x1, _ = squares(close_kernel, "close", 3, 1, *state)
    zero = jnp.zeros_like(l0)
    x10 = -jnp.dot(x1, jnp.dot(l10, x0, precision="highest"), precision="highest")
    return jnp.block([[l0, zero], [l10, l1]]), jnp.block([[x0, zero], [x10, x1]])


def solve_kernel(col_ref, g0, g1, inv0, inv0_t, below, below_t, inv1, inv1_t, wh, wl, y, mid):
    col = col_ref[0]
    half = NB // 2
    y0 = jnp.concatenate([dot3(inv0[0:half, 0:half], g0[0:half, :]), dot3(inv0[half:, :], g0[...])], axis=0)
    rest = g1[...] - dot3(below[...], y0)
    y1 = jnp.concatenate([dot3(inv1[0:half, 0:half], rest[0:half, :]), dot3(inv1[half:, :], rest)], axis=0)
    rows = lax.broadcasted_iota(jnp.int32, (NB, NB), 0)
    lanes = lax.broadcasted_iota(jnp.int32, (NB, NB), 1)
    y[0:NB, :] = y0[:, NB:]
    y[NB:, :] = y1[:, NB:]
    unit = jnp.where(rows == lanes, F32(-1), F32(0))
    mid[0:NB, NB:] = y0[:, NB:]
    mid[NB:, NB:] = y1[:, NB:]
    mid[0:NB, 0:NB] = jnp.where(col == 0, unit, jnp.where(col == 1, F32(0), y0[:, 0:NB]))
    mid[NB:, 0:NB] = jnp.where(col == 1, unit, jnp.where(col == 0, F32(0), y1[:, 0:NB]))
    w1 = jnp.concatenate(
        [dot3(inv1_t[0:half, :], mid[NB:, :]), dot3(inv1_t[half:, half:], mid[NB + half :, :])], axis=0
    )
    h, l = split(w1)
    wh[NB:, :] = h
    wl[NB:, :] = l
    z0 = mid[0:NB, :] - dot3(below_t[...], w1)
    w0 = jnp.concatenate([dot3(inv0_t[0:half, :], z0), dot3(inv0_t[half:, half:], z0[half:, :])], axis=0)
    h, l = split(w0)
    wh[0:NB, :] = h
    wl[0:NB, :] = l


def update_kernel(place, wh, wl, special, y, *refs):
    a_refs, b_refs = refs[0:5], refs[5:10]
    mat, rhs, out, out_rhs, rbuf, mbuf, vbuf, obuf, qbuf, rsem, msem, vsem, osem, qsem = refs[10:]
    row, col, here_z, here_y = place[0], place[1], place[2], place[3]
    steps = 8

    def chunk(s, k):
        z = (here_z + jnp.where(s < 4, s, k)) % 4
        v = (here_y + jnp.where(s < 4, k, s - 4)) % 4
        return pl.multiple_of((z * 4 + v) * 2 * TILE + jnp.where(s < 4, 0, TILE), TILE)

    def load(s, slot):
        for t in range(steps):
            refs5 = a_refs if t < 4 else b_refs
            own, plus, minus, far0, far1 = refs5

            @pl.when(s == t)
            def _(t=t, own=own, plus=plus, minus=minus, far0=far0, far1=far1):
                if t % 4 == 2:
                    pltpu.make_async_copy(far0, rbuf.at[slot, pl.ds(0, NB // 2)], rsem.at[slot]).start()
                    pltpu.make_async_copy(far1, rbuf.at[slot, pl.ds(NB // 2, NB // 2)], rsem.at[slot]).start()
                else:
                    pltpu.make_async_copy((own, plus, None, minus)[t % 4], rbuf.at[slot], rsem.at[slot]).start()

        for k in range(4):
            at = chunk(s, k)
            pltpu.make_async_copy(mat.at[pl.ds(at, TILE)], mbuf.at[slot, pl.ds(k * TILE, TILE)], msem.at[slot]).start()
            pltpu.make_async_copy(rhs.at[pl.ds(at, TILE)], vbuf.at[slot, pl.ds(k * TILE, TILE)], vsem.at[slot]).start()

    def drain(slot):
        pltpu.make_async_copy(obuf.at[slot], obuf.at[slot], osem.at[slot]).wait()
        pltpu.make_async_copy(qbuf.at[slot], qbuf.at[slot], qsem.at[slot]).wait()

    mul = lambda p, q: lax.dot_general(p, q, NN, preferred_element_type=F32)
    load(0, 0)

    def step(s, carry):
        slot = s % 2

        @pl.when(s + 1 < steps)
        def _():
            load(s + 1, 1 - slot)

        pltpu.make_async_copy(rbuf.at[slot], rbuf.at[slot], rsem.at[slot]).wait()
        pltpu.make_async_copy(mbuf.at[slot], mbuf.at[slot], msem.at[slot]).wait()
        pltpu.make_async_copy(vbuf.at[slot], vbuf.at[slot], vsem.at[slot]).wait()

        @pl.when(s >= 2)
        def _():
            drain(slot)

        rh, rl = split(rbuf[slot])
        acc = mul(rh, wh[...]) + (mul(rh, wl[...]) + mul(rl, wh[...]))
        obuf[slot] = jnp.where(col < 2, F32(0), mbuf[slot]) - acc[:, 0:NB]
        qbuf[slot] = vbuf[slot] - acc[:, NB:]
        for k in range(4):
            at = chunk(s, k)

            @pl.when(jnp.logical_and(row < 2, at < NB))
            def _():
                obuf[slot, pl.ds(k * TILE, TILE), :] = special[pl.ds(pl.multiple_of(at % NB, TILE), TILE), :]
                qbuf[slot, pl.ds(k * TILE, TILE), :] = y[pl.ds(pl.multiple_of(at % NB, TILE), TILE), :]

            pltpu.make_async_copy(obuf.at[slot, pl.ds(k * TILE, TILE)], out.at[pl.ds(at, TILE)], osem.at[slot]).start()
            pltpu.make_async_copy(
                qbuf.at[slot, pl.ds(k * TILE, TILE)], out_rhs.at[pl.ds(at, TILE)], qsem.at[slot]
            ).start()
        return carry

    lax.fori_loop(0, steps, step, 0)
    drain(0)
    drain(1)


def ordered(parts, first):
    both = jnp.concatenate(parts + parts, axis=0)
    size = parts[0].shape[0]
    return lax.dynamic_slice_in_dim(both, (4 - first) % 4 * size, 4 * size, 0)


def turn_kernel(source, target):
    target[...] = source[...].T


def turn(value):
    return pl.pallas_call(
        turn_kernel,
        out_shape=jax.ShapeDtypeStruct(value.shape, F32),
        in_specs=[VMEM],
        out_specs=VMEM,
        compiler_params=pltpu.CompilerParams(vmem_limit_bytes=8 << 20),
        cost_estimate=pl.CostEstimate(flops=0, bytes_accessed=2 << 20, transcendentals=0),
        name="turn",
    )(value)


def ring(axis, d):
    if axis == "y":
        return lambda X, Y, Z, C: (X, Y - d, Z, C)
    return lambda X, Y, Z, C: (X, Y, Z - d, C)


def tie(*values):
    return lax.optimization_barrier(values)


def body(matrix, right_sides):
    row = lax.axis_index("row")
    col = lax.axis_index("col")
    core, x_lo = row % 2, row // 2
    z, y, x = col // 8, col // 2 % 4, col % 2 * 2 + row // 2
    first = matrix[0:NB]

    part, half = NB // 4, NB // 2
    turned = turn(first)

    recv = []
    for d in (1, 2, 3):
        block = jnp.where(x == 2, (2 + d) % 4, d)
        recv.append(
            send(
                lax.dynamic_slice_in_dim(first, block * part, part, 0),
                lambda X, Y, Z, C, d=d: (X + d, Y, Z, C) if (Y, Z) == (0, 0) and X % 2 == 0 else None,
            )
        )
    here = lax.dynamic_slice_in_dim(first, x * part, part, 0)
    r1, r2, r3 = recv
    main = jnp.where(x == 0, here, jnp.where(x == 1, r1, jnp.where(x == 2, r2, r3)))
    corner = jnp.where(x == 0, r2, jnp.where(x == 1, r3, jnp.where(x == 2, here, r1)))
    held, turned = tie(jnp.concatenate([main, corner], axis=0), turned)

    def strew(m):
        def rule(X, Y, Z, C):
            if X % 2:
                return None
            u, v = m // 2 ^ C, m % 2 ^ C
            return (2 * (X // 2 ^ v) + Y % 2, Y // 2 * 2 + (Y % 2 ^ u), Z, X // 2)

        h = jnp.bitwise_xor(jnp.bitwise_xor(y % 2, m // 2), core)
        return send(lax.dynamic_slice_in_dim(turned, h * half, half, 0), rule)

    small = held.shape[0] // 4
    mine = jnp.where(z == 0, held[0:small], F32(0))
    for d in (1, 2, 3):
        mine = mine + send(
            held[d * small : (d + 1) * small], lambda X, Y, Z, C, d=d: (X, Y, d, C) if (Y, Z) == (0, 0) else None
        )
    got = [strew(0), strew(1)]
    mine, turned, *got = tie(mine, turned, *got)

    every = jnp.where(y == 0, mine, F32(0))
    for d in (1, 2, 3):
        every = every + send(mine, lambda X, Y, Z, C, d=d: (X, d, Z, C) if Y == 0 else None)
    got += [strew(2), strew(3)]
    every, *got = tie(every, *got)

    zs = [every] + [send(every, ring("z", d)) for d in (1, 2, 3)]
    u = jnp.bitwise_xor(y % 2, x % 2)
    v = jnp.bitwise_xor(x // 2, core)
    pick = lambda a, b, p: jnp.where(a == 0, jnp.where(b == 0, p[0], p[1]), jnp.where(b == 0, p[2], p[3]))
    piece = jnp.concatenate([pick(u, v, got), pick(1 - u, 1 - v, got)], axis=1)
    piece_a, piece_b = piece[0:TILE], piece[TILE:]
    a1, a3 = send(piece_a, ring("y", 1)), send(piece_a, ring("y", 3))
    ring_z = ordered(zs, z)
    ring_z, piece_a, piece_b, a1, a3 = tie(ring_z, piece_a, piece_b, a1, a3)

    mains = [ring_z[0:part]] + [send(ring_z[0:part], lambda X, Y, Z, C, d=d: (X - d, Y, Z, C)) for d in (1, 2, 3)]
    a2, b1 = send(piece_a, ring("y", 2)), send(piece_b, ring("z", 1))
    main = ordered(mains, x)
    main, a2, b1, piece_b = tie(main, a2, b1, piece_b)
    other_main = swap_cores(main)
    b3, b2 = send(piece_b, ring("z", 3)), send(piece_b, ring("z", 2))
    a00 = jnp.where(core == 0, main, other_main)
    a10 = jnp.where(core == 0, other_main, main)
    tail = ring_z[part:]
    a00, tail = tie(a00, tail)
    corners = [tail] + [send(tail, lambda X, Y, Z, C, d=d: (X - d, Y, Z, C)) for d in (1, 2, 3)]

    state = squares(open_kernel, "open0", 4, 0, a00)

    state, b2, b3, corners = tie(state, b2, b3, corners)
    corner = ordered(corners, x)
    other_corner = swap_cores(corner)
    a11 = jnp.where(core == 0, other_corner, corner)
    rows_a = jnp.concatenate([piece_a, a1, a2, a3], axis=0)
    rows_b = jnp.concatenate([piece_b, b1, b2, b3], axis=0)
    fars = []
    for rows, axis in ((rows_a, "z"), (rows_b, "y")):
        fars.append((send(rows, ring(axis, 1)), send(rows, ring(axis, 3))))
    first_rows, top_rhs, a11 = tie(first, right_sides[0:NB], a11)

    top = jnp.concatenate([first_rows, top_rhs], axis=1)
    crossed = send(top, lambda X, Y, Z, C: (X + 1, Y, Z, C) if X % 2 == 0 else None)
    l0, inv0, inv0_t, below, below_t, rest = squares(below_kernel, "below0", 6, 1, *state, a10, a11)
    state = squares(open_kernel, "open1", 4, 0, rest)

    state, fars, crossed = tie(state, fars, crossed)
    own = jnp.where(x_lo == 0, top, crossed)
    partner = swap_cores(own)
    gathered = []
    for (plus, minus), rows, axis in ((fars[0], rows_a, "z"), (fars[1], rows_b, "y")):
        far0 = send(plus[0:half], ring(axis, 1))
        far1 = send(minus[half:], ring(axis, 3))
        gathered += [rows, plus, minus, far0, far1]

    l1, inv1, inv1_t = squares(close_kernel, "close1", 3, 1, *state)
    g0 = jnp.where(core == 0, own, partner)
    g1 = jnp.where(core == 0, partner, own)

    width = NB + right_sides.shape[1]
    wh, wl, answer = pl.pallas_call(
        solve_kernel,
        out_shape=(
            jax.ShapeDtypeStruct((EDGE, width), BF16),
            jax.ShapeDtypeStruct((EDGE, width), BF16),
            jax.ShapeDtypeStruct((EDGE, width - NB), F32),
        ),
        in_specs=[pl.BlockSpec(memory_space=pltpu.SMEM)] + [VMEM] * 8,
        out_specs=(VMEM,) * 3,
        scratch_shapes=[pltpu.VMEM((EDGE, width), F32)],
        compiler_params=pltpu.CompilerParams(vmem_limit_bytes=48 << 20),
        cost_estimate=pl.CostEstimate(flops=10_000_000_000, bytes_accessed=16 << 20, transcendentals=0),
        name="solve",
    )(col.reshape(1), g0, g1, inv0, inv0_t, below, below_t, inv1, inv1_t)

    lower = jnp.where(row == 0, jnp.where(col == 0, l0, F32(0)), jnp.where(col == 0, below, l1))
    special = jnp.where(col < 2, lower, F32(0))
    answer = lax.dynamic_slice_in_dim(answer, row % 2 * NB, NB, 0)

    anywhere = pl.BlockSpec(memory_space=pl.ANY)
    pair = lambda *shape: pltpu.VMEM((2,) + shape, F32)
    return pl.pallas_call(
        update_kernel,
        in_specs=[pl.BlockSpec(memory_space=pltpu.SMEM)] + [VMEM] * 4 + [anywhere] * 12,
        out_specs=(anywhere, anywhere),
        out_shape=(
            jax.ShapeDtypeStruct(matrix.shape, F32),
            jax.ShapeDtypeStruct(right_sides.shape, F32),
        ),
        scratch_shapes=[
            pair(NB, EDGE),
            pair(NB, NB),
            pair(NB, width - NB),
            pair(NB, NB),
            pair(NB, width - NB),
        ]
        + [pltpu.SemaphoreType.DMA((2,))] * 5,
        compiler_params=pltpu.CompilerParams(vmem_limit_bytes=48 << 20),
        cost_estimate=pl.CostEstimate(flops=20_000_000_000, bytes_accessed=44 << 20, transcendentals=0),
        name="update",
    )(jnp.stack([row, col, z, y]), wh, wl, special, answer, *gathered, matrix, right_sides)


def solution(mesh):
    specs = (P("row", "col"), P("row", None))
    return jax.shard_map(body, mesh=mesh, in_specs=specs, out_specs=specs, check_vma=False)
```

```python
import functools
import jax
import jax.numpy as jnp
from jax import lax
from jax.experimental import pallas as pl
from jax.experimental.pallas import tpu as pltpu
from jax.sharding import PartitionSpec as P

NB = 512
EDGE = 1024
TILE = 128
AXES = ("row", "col")
F32 = jnp.float32
BF16 = jnp.bfloat16
NN = (((1,), (0,)), ((), ()))
NT = (((1,), (1,)), ((), ()))
VMEM = pl.BlockSpec(memory_space=pltpu.VMEM)


def device_index(x, y, z, core):
    return ((x % 2) * 2 + core) * 32 + (z % 4) * 8 + (y % 4) * 2 + (x % 4) // 2


def route(rule):
    pairs = []
    for x in range(4):
        for y in range(4):
            for z in range(4):
                for core in range(2):
                    target = rule(x, y, z, core)
                    if target is not None:
                        pairs.append((device_index(x, y, z, core), device_index(*target)))
    return pairs


def send(value, rule):
    return lax.ppermute(value, AXES, route(rule))


def swap_cores(value):
    return send(value, lambda x, y, z, c: (x, y, z, 1 - c))


def split(value):
    high = value.astype(BF16)
    return high, (value - high.astype(F32)).astype(BF16)


def dot3(a, b, dims=NN):
    ah, al = split(a)
    bh, bl = split(b)
    mul = lambda p, q: lax.dot_general(p, q, dims, preferred_element_type=F32)
    return mul(ah, bh) + (mul(ah, bl) + mul(al, bh))


def dot_full(a, b, dims=NN):
    return lax.dot_general(a, b, dims, precision=lax.Precision.HIGHEST, preferred_element_type=F32)


def factor_tile(work, inverse, factor_t):
    rows = lax.broadcasted_iota(jnp.int32, (TILE, TILE), 0)
    lanes = lax.broadcasted_iota(jnp.int32, (TILE, TILE), 1)
    inverse[...] = jnp.where(rows == lanes, F32(1), F32(0))
    lane8 = lax.broadcasted_iota(jnp.int32, (8, TILE), 1)
    row8 = lax.broadcasted_iota(jnp.int32, (8, TILE), 0)
    spread = lambda v, s: jnp.broadcast_to(v[:, s : s + 1], (8, TILE))
    tile = lambda g: pl.ds(pl.multiple_of(g % 16 * 8, 8), 8)

    def pivot(g, top, cols, eye, below, below_eye):
        whole = lambda v, t: jnp.broadcast_to(v[t : t + 1, :], (8, TILE))
        e = [[whole(cols[s], t) if s <= t else None for s in range(8)] for t in range(8)]
        low = [[None] * 8 for _ in range(8)]
        scale = [None] * 8
        for s in range(8):
            scale[s] = r = lax.rsqrt(e[s][s])
            for t in range(s + 1, 8):
                low[t][s] = e[t][s] * r
            for u in range(s + 1, 8):
                for t in range(u, 8):
                    e[t][u] = e[t][u] - low[t][s] * low[u][s]
        inv = [[None] * 8 for _ in range(8)]
        for s in range(8):
            inv[s][s] = scale[s]
            for t in range(s + 1, 8):
                total = low[t][s] * inv[s][s]
                for u in range(s + 1, t):
                    total = total + low[t][u] * inv[u][s]
                inv[t][s] = -total * scale[t]
        upper = None
        solved = None
        for t in range(8):
            column = jnp.where(row8 == t, inv[t][t], F32(0))
            for s in range(t + 1, 8):
                column = jnp.where(row8 == s, inv[s][t], column)
            a = column * top[t : t + 1, :]
            b = column * eye[t : t + 1, :]
            upper = a if upper is None else upper + a
            solved = b if solved is None else solved + b
        upper = jnp.where(lane8 < TILE - 8 * g, upper, F32(0))
        back = None
        for s in range(8):
            column = jnp.where(row8 == s, inv[s][s], F32(0))
            for t in range(s):
                column = jnp.where(row8 == t, inv[s][t], column)
            a = column * upper[s : s + 1, :]
            b = column * solved[s : s + 1, :]
            back = (a, b) if back is None else (back[0] + a, back[1] + b)
        below, below_eye = apply(below, below_eye, back)
        cols = tuple(spread(below, 8 + s) for s in range(8))
        return upper, solved, back, pltpu.roll(below, TILE - 8, 1), below_eye, cols

    def apply(new, row, back):
        mults = [spread(new, s) for s in range(8)]
        for s in range(8):
            new = new - mults[s] * back[0][s : s + 1, :]
            row = row - mults[s] * back[1][s : s + 1, :]
        return new, row

    def group(last, g, carry):
        back, top, eye, cols = carry
        below, below_eye = apply(work[16:24, :], inverse[tile(g + 2), :], back)
        for q in range(3, last):
            new, row = apply(work[8 * q : 8 * q + 8, :], inverse[tile(g + q), :], back)
            work[8 * q - 8 : 8 * q, :] = pltpu.roll(new, TILE - 8, 1)
            inverse[tile(g + q), :] = row
        work[8 * last - 8 : 8 * last, :] = jnp.zeros((8, TILE), F32)
        carry = pivot(g + 1, top, cols, eye, pltpu.roll(below, TILE - 8, 1), below_eye)
        factor_t[tile(g + 1), :] = pltpu.roll(carry[0], 8 * (g + 1), 1)
        inverse[tile(g + 1), :] = carry[1]
        return carry[2:]

    top = work[0:8, :]
    cols = tuple(spread(top, s) for s in range(8))
    carry = pivot(0, top, cols, inverse[0:8, :], work[8:16, :], inverse[8:16, :])
    factor_t[0:8, :] = carry[0]
    inverse[0:8, :] = carry[1]
    carry = carry[2:]
    for first, stop, last in ((0, 3, 16), (3, 6, 13), (6, 9, 10), (9, 12, 7), (12, 15, 4)):
        carry = lax.fori_loop(first, stop, functools.partial(group, last), carry)


def factor_blocks(blocks, mat, low, inv, inv_t, work, tile_inv, tile_t):
    rows = lax.broadcasted_iota(jnp.int32, (TILE, TILE), 0)
    lanes = lax.broadcasted_iota(jnp.int32, (TILE, TILE), 1)
    for b in blocks:
        s, e = b * TILE, (b + 1) * TILE
        work[...] = mat[s:e, s:e]
        factor_tile(work, tile_inv, tile_t)
        x = jnp.where(rows >= lanes, tile_inv[...], F32(0))
        low[s:e, s:e] = jnp.where(rows >= lanes, tile_t[...].T, F32(0))
        inv[s:e, s:e] = x
        inv_t[s:e, s:e] = x.T
        if b > 0:
            left = dot_full(low[s:e, 0:s], inv[0:s, 0:s])
            left = -dot_full(x, left)
            inv[s:e, 0:s] = left
            inv_t[0:s, s:e] = left.T
        if e < NB:
            panel = dot_full(mat[e:NB, s:e], x, NT)
            low[e:NB, s:e] = panel
            for c in range(e, NB, 2 * TILE):
                d = min(c + 2 * TILE, NB)
                mat[c:NB, c:d] = mat[c:NB, c:d] - dot_full(panel[c - e :], panel[c - e : d - e], NT)


def place_quarters(place, mine, other, target, core):
    quarter = NB // 4
    for d in range(4):
        at = pl.multiple_of((place[0] + d) % 4 * quarter, quarter)
        rows = slice(d * quarter, (d + 1) * quarter)
        target[pl.ds(at, quarter), :] = jnp.where(place[1] == core, mine[rows, :], other[rows, :])


def first_kernel(place, mine, other, mat, low, inv, inv_t, work, tile_inv, tile_t):
    place_quarters(place, mine, other, mat, 0)
    low[...] = jnp.zeros_like(low)
    inv[...] = jnp.zeros_like(inv)
    inv_t[...] = jnp.zeros_like(inv_t)
    factor_blocks((0, 1), mat, low, inv, inv_t, work, tile_inv, tile_t)


def open_kernel(source, mat, low, inv, inv_t, work, tile_inv, tile_t):
    mat[...] = source[...]
    low[...] = jnp.zeros_like(low)
    inv[...] = jnp.zeros_like(inv)
    inv_t[...] = jnp.zeros_like(inv_t)
    factor_blocks((0, 1), mat, low, inv, inv_t, work, tile_inv, tile_t)


def carry_on(sources, mat, low, inv, inv_t, tiles):
    for source, target in zip(sources, (mat, low, inv, inv_t)):
        target[...] = source[...]
    factor_blocks((2, 3), mat, low, inv, inv_t, *tiles)


def close_kernel(m, l, i, t, low, inv, inv_t, mat, *tiles):
    carry_on((m, l, i, t), mat, low, inv, inv_t, tiles)


def below_kernel(place, m, l, i, t, mine, other, edge, far_edge, low, inv, inv_t, below, below_t, rest, mat, *tiles):
    carry_on((m, l, i, t), mat, low, inv, inv_t, tiles)
    place_quarters(place, mine, other, rest, 1)
    panel = dot_full(rest[...], inv_t[...])
    below[...] = panel
    below_t[...] = panel.T
    place_quarters(place, edge, far_edge, rest, 1)
    rest[...] = rest[...] - dot_full(panel, panel, NT)


def squares(kernel, name, outs, held, *args, place=()):
    return pl.pallas_call(
        kernel,
        out_shape=(jax.ShapeDtypeStruct((NB, NB), F32),) * outs,
        in_specs=[pl.BlockSpec(memory_space=pltpu.SMEM)] * len(place) + [VMEM] * len(args),
        out_specs=(VMEM,) * outs,
        scratch_shapes=[pltpu.VMEM((NB, NB), F32)] * held + [pltpu.VMEM((TILE, TILE), F32)] * 3,
        compiler_params=pltpu.CompilerParams(vmem_limit_bytes=24 << 20),
        cost_estimate=pl.CostEstimate(flops=30_000_000_000, bytes_accessed=len(args) << 20, transcendentals=0),
        name=name,
    )(*place, *args)


def solve_kernel(col_ref, g0, g1, inv0, inv0_t, below, below_t, inv1, inv1_t, parts, y, mid):
    col = col_ref[0]

    def put(at, value):
        high, low = split(value)
        for k, part in enumerate((high, low, high)):
            parts[k * EDGE + at : k * EDGE + at + NB, :] = part

    half = NB // 2
    y0 = jnp.concatenate([dot3(inv0[0:half, 0:half], g0[0:half, :]), dot3(inv0[half:, :], g0[...])], axis=0)
    rest = g1[...] - dot3(below[...], y0)
    y1 = jnp.concatenate([dot3(inv1[0:half, 0:half], rest[0:half, :]), dot3(inv1[half:, :], rest)], axis=0)
    rows = lax.broadcasted_iota(jnp.int32, (NB, NB), 0)
    lanes = lax.broadcasted_iota(jnp.int32, (NB, NB), 1)
    y[0:NB, :] = y0[:, NB:]
    y[NB:, :] = y1[:, NB:]
    unit = jnp.where(rows == lanes, F32(-1), F32(0))
    mid[0:NB, NB:] = y0[:, NB:]
    mid[NB:, NB:] = y1[:, NB:]
    mid[0:NB, 0:NB] = jnp.where(col == 0, unit, jnp.where(col == 1, F32(0), y0[:, 0:NB]))
    mid[NB:, 0:NB] = jnp.where(col == 1, unit, jnp.where(col == 0, F32(0), y1[:, 0:NB]))
    w1 = jnp.concatenate(
        [dot3(inv1_t[0:half, :], mid[NB:, :]), dot3(inv1_t[half:, half:], mid[NB + half :, :])], axis=0
    )
    put(NB, w1)
    z0 = mid[0:NB, :] - dot3(below_t[...], w1)
    w0 = jnp.concatenate([dot3(inv0_t[0:half, :], z0), dot3(inv0_t[half:, half:], z0[half:, :])], axis=0)
    put(0, w0)


def update_kernel(place, weights, special, y, *refs):
    a_refs, b_refs = refs[0:5], refs[5:10]
    mat, rhs, out, out_rhs, rbuf, mbuf, vbuf, obuf, qbuf, rsem, msem, vsem, osem, qsem = refs[10:]
    row, col, here_z, here_y = place[0], place[1], place[2], place[3]
    steps = 8

    def chunk(s, k):
        z = (here_z + jnp.where(s < 4, s, k)) % 4
        v = (here_y + jnp.where(s < 4, k, s - 4)) % 4
        return pl.multiple_of((z * 4 + v) * 2 * TILE + jnp.where(s < 4, 0, TILE), TILE)

    def load(s, slot):
        for t in range(steps):
            refs5 = a_refs if t < 4 else b_refs
            own, plus, minus, far0, far1 = refs5

            @pl.when(s == t)
            def _(t=t, own=own, plus=plus, minus=minus, far0=far0, far1=far1):
                if t % 4 == 2:
                    pltpu.make_async_copy(far0, rbuf.at[slot, pl.ds(0, NB // 2)], rsem.at[slot]).start()
                    pltpu.make_async_copy(far1, rbuf.at[slot, pl.ds(NB // 2, NB // 2)], rsem.at[slot]).start()
                else:
                    pltpu.make_async_copy((own, plus, None, minus)[t % 4], rbuf.at[slot], rsem.at[slot]).start()

        for k in range(4):
            at = chunk(s, k)
            pltpu.make_async_copy(mat.at[pl.ds(at, TILE)], mbuf.at[slot, pl.ds(k * TILE, TILE)], msem.at[slot]).start()
            pltpu.make_async_copy(rhs.at[pl.ds(at, TILE)], vbuf.at[slot, pl.ds(k * TILE, TILE)], vsem.at[slot]).start()

    def drain(slot):
        pltpu.make_async_copy(obuf.at[slot], obuf.at[slot], osem.at[slot]).wait()
        pltpu.make_async_copy(qbuf.at[slot], qbuf.at[slot], qsem.at[slot]).wait()

    mul = lambda p, q: lax.dot_general(p, q, NN, preferred_element_type=F32)
    load(0, 0)

    def step(s, carry):
        slot = s % 2

        @pl.when(s + 1 < steps)
        def _():
            load(s + 1, 1 - slot)

        pltpu.make_async_copy(rbuf.at[slot], rbuf.at[slot], rsem.at[slot]).wait()
        pltpu.make_async_copy(mbuf.at[slot], mbuf.at[slot], msem.at[slot]).wait()
        pltpu.make_async_copy(vbuf.at[slot], vbuf.at[slot], vsem.at[slot]).wait()

        @pl.when(s >= 2)
        def _():
            drain(slot)

        rh, rl = split(rbuf[slot])
        acc = mul(jnp.concatenate([rh, rh, rl], axis=1), weights[...])
        obuf[slot] = jnp.where(col < 2, F32(0), mbuf[slot]) - acc[:, 0:NB]
        qbuf[slot] = vbuf[slot] - acc[:, NB:]
        for k in range(4):
            at = chunk(s, k)

            @pl.when(jnp.logical_and(row < 2, at < NB))
            def _():
                obuf[slot, pl.ds(k * TILE, TILE), :] = special[pl.ds(pl.multiple_of(at % NB, TILE), TILE), :]
                qbuf[slot, pl.ds(k * TILE, TILE), :] = y[pl.ds(pl.multiple_of(at % NB, TILE), TILE), :]

            pltpu.make_async_copy(obuf.at[slot, pl.ds(k * TILE, TILE)], out.at[pl.ds(at, TILE)], osem.at[slot]).start()
            pltpu.make_async_copy(
                qbuf.at[slot, pl.ds(k * TILE, TILE)], out_rhs.at[pl.ds(at, TILE)], qsem.at[slot]
            ).start()
        return carry

    lax.fori_loop(0, steps, step, 0)
    drain(0)
    drain(1)


def ordered(parts, first):
    return jnp.concatenate([lax.select_n(first, *(parts[(m - f) % 4] for f in range(4))) for m in range(4)], axis=0)


def join_kernel(*refs):
    parts, (first, second), sems = refs[:8], refs[8:10], refs[10]
    copies = []
    for k in range(8):
        target = (first, second)[k // 4].at[pl.ds(k % 4 * TILE, TILE)]
        copies.append(pltpu.make_async_copy(parts[k], target, sems.at[k]))
    for copy in copies:
        copy.start()
    for copy in copies:
        copy.wait()


def join(*parts):
    anywhere = pl.BlockSpec(memory_space=pl.ANY)
    return pl.pallas_call(
        join_kernel,
        out_shape=(jax.ShapeDtypeStruct((4 * TILE, EDGE), F32),) * 2,
        in_specs=[anywhere] * 8,
        out_specs=(anywhere,) * 2,
        scratch_shapes=[pltpu.SemaphoreType.DMA((8,))],
        cost_estimate=pl.CostEstimate(flops=0, bytes_accessed=8 << 20, transcendentals=0),
        name="join",
    )(*parts)


def turn_kernel(source, target):
    target[...] = source[...].T


def turn(value):
    return pl.pallas_call(
        turn_kernel,
        out_shape=jax.ShapeDtypeStruct(value.shape, F32),
        in_specs=[VMEM],
        out_specs=VMEM,
        compiler_params=pltpu.CompilerParams(vmem_limit_bytes=8 << 20),
        cost_estimate=pl.CostEstimate(flops=0, bytes_accessed=2 << 20, transcendentals=0),
        name="turn",
    )(value)


def ring(axis, d):
    if axis == "y":
        return lambda X, Y, Z, C: (X, Y - d, Z, C)
    return lambda X, Y, Z, C: (X, Y, Z - d, C)


def tie(*values):
    return lax.optimization_barrier(values)


def body(matrix, right_sides):
    row = lax.axis_index("row")
    col = lax.axis_index("col")
    core, x_lo = row % 2, row // 2
    z, y, x = col // 8, col // 2 % 4, col % 2 * 2 + row // 2
    first = matrix[0:NB]

    part, half = NB // 4, NB // 2
    turned = turn(first)

    recv = []
    for d in (1, 2, 3):
        block = jnp.where(x == 2, (2 + d) % 4, d)
        recv.append(
            send(
                lax.dynamic_slice_in_dim(first, block * part, part, 0),
                lambda X, Y, Z, C, d=d: (X + d, Y, Z, C) if (Y, Z) == (0, 0) and X % 2 == 0 else None,
            )
        )
    here = lax.dynamic_slice_in_dim(first, x * part, part, 0)
    r1, r2, r3 = recv
    main = jnp.where(x == 0, here, jnp.where(x == 1, r1, jnp.where(x == 2, r2, r3)))
    corner = jnp.where(x == 0, r2, jnp.where(x == 1, r3, jnp.where(x == 2, here, r1)))
    held, turned = tie(jnp.concatenate([main, corner], axis=0), turned)

    def strew(m):
        def rule(X, Y, Z, C):
            if X % 2:
                return None
            u, v = m // 2 ^ C, m % 2 ^ C
            return (2 * (X // 2 ^ v) + Y % 2, Y // 2 * 2 + (Y % 2 ^ u), Z, X // 2)

        h = jnp.bitwise_xor(jnp.bitwise_xor(y % 2, m // 2), core)
        return send(lax.dynamic_slice_in_dim(turned, h * half, half, 0), rule)

    small = held.shape[0] // 4
    mine = jnp.where(z == 0, held[0:small], F32(0))
    for d in (1, 2, 3):
        mine = mine + send(
            held[d * small : (d + 1) * small], lambda X, Y, Z, C, d=d: (X, Y, d, C) if (Y, Z) == (0, 0) else None
        )
    got = [strew(0), strew(1)]
    mine, turned, *got = tie(mine, turned, *got)

    every = jnp.where(y == 0, mine, F32(0))
    for d in (1, 2, 3):
        every = every + send(mine, lambda X, Y, Z, C, d=d: (X, d, Z, C) if Y == 0 else None)
    got += [strew(2), strew(3)]
    (every,) = tie(every)

    zs = [every] + [send(every, ring("z", d)) for d in (1, 2, 3)]
    u = jnp.bitwise_xor(y % 2, x % 2)
    v = jnp.bitwise_xor(x // 2, core)
    pick = lambda a, b, p: jnp.where(a == 0, jnp.where(b == 0, p[0], p[1]), jnp.where(b == 0, p[2], p[3]))
    piece = jnp.concatenate([pick(u, v, got), pick(1 - u, 1 - v, got)], axis=1)
    piece_a, piece_b = piece[0:TILE], piece[TILE:]
    ring_z = ordered(zs, z)
    ring_z, piece_a, piece_b = tie(ring_z, piece_a, piece_b)

    mains = [ring_z[0:part]] + [send(ring_z[0:part], lambda X, Y, Z, C, d=d: (X - d, Y, Z, C)) for d in (1, 2, 3)]
    a1, a3 = send(piece_a, ring("y", 1)), send(piece_a, ring("y", 3))
    main = jnp.concatenate(mains, axis=0)
    main, a1, a3, piece_a, piece_b = tie(main, a1, a3, piece_a, piece_b)
    other_main = swap_cores(main)
    a2, b1 = send(piece_a, ring("y", 2)), send(piece_b, ring("z", 1))
    tail = ring_z[part:]
    main, other_main, tail, a2, b1, piece_b = tie(main, other_main, tail, a2, b1, piece_b)
    corners = [tail] + [send(tail, lambda X, Y, Z, C, d=d: (X - d, Y, Z, C)) for d in (1, 2, 3)]
    b2, b3 = send(piece_b, ring("z", 2)), send(piece_b, ring("z", 3))

    place = (jnp.stack([x, core]),)
    state = squares(first_kernel, "open0", 4, 0, main, other_main, place=place)

    state, b2, b3, corners = tie(state, b2, b3, corners)
    corner = jnp.concatenate(corners, axis=0)
    other_corner = swap_cores(corner)
    rows_a, rows_b = join(piece_a, a1, a2, a3, piece_b, b1, b2, b3)
    fars = []
    for rows, axis in ((rows_a, "z"), (rows_b, "y")):
        fars.append((send(rows, ring(axis, 1)), send(rows, ring(axis, 3))))
    first_rows, top_rhs, other_corner = tie(first, right_sides[0:NB], other_corner)

    top = jnp.concatenate([first_rows, top_rhs], axis=1)
    crossed = send(top, lambda X, Y, Z, C: (X + 1, Y, Z, C) if X % 2 == 0 else None)
    l0, inv0, inv0_t, below, below_t, rest = squares(
        below_kernel, "below0", 6, 1, *state, main, other_main, corner, other_corner, place=place
    )
    state = squares(open_kernel, "open1", 4, 0, rest)

    state, fars, crossed = tie(state, fars, crossed)
    own = jnp.where(x_lo == 0, top, crossed)
    partner = swap_cores(own)
    gathered = []
    for (plus, minus), rows, axis in ((fars[0], rows_a, "z"), (fars[1], rows_b, "y")):
        far0 = send(plus[0:half], ring(axis, 1))
        far1 = send(minus[half:], ring(axis, 3))
        gathered += [rows, plus, minus, far0, far1]

    l1, inv1, inv1_t = squares(close_kernel, "close1", 3, 1, *state)
    g0 = jnp.where(core == 0, own, partner)
    g1 = jnp.where(core == 0, partner, own)

    width = NB + right_sides.shape[1]
    weights, answer = pl.pallas_call(
        solve_kernel,
        out_shape=(
            jax.ShapeDtypeStruct((3 * EDGE, width), BF16),
            jax.ShapeDtypeStruct((EDGE, width - NB), F32),
        ),
        in_specs=[pl.BlockSpec(memory_space=pltpu.SMEM)] + [VMEM] * 8,
        out_specs=(VMEM,) * 2,
        scratch_shapes=[pltpu.VMEM((EDGE, width), F32)],
        compiler_params=pltpu.CompilerParams(vmem_limit_bytes=48 << 20),
        cost_estimate=pl.CostEstimate(flops=10_000_000_000, bytes_accessed=16 << 20, transcendentals=0),
        name="solve",
    )(col.reshape(1), g0, g1, inv0, inv0_t, below, below_t, inv1, inv1_t)

    lower = jnp.where(row == 0, jnp.where(col == 0, l0, F32(0)), jnp.where(col == 0, below, l1))
    special = jnp.where(col < 2, lower, F32(0))
    answer = lax.dynamic_slice_in_dim(answer, row % 2 * NB, NB, 0)

    anywhere = pl.BlockSpec(memory_space=pl.ANY)
    pair = lambda *shape: pltpu.VMEM((2,) + shape, F32)
    return pl.pallas_call(
        update_kernel,
        in_specs=[pl.BlockSpec(memory_space=pltpu.SMEM)] + [VMEM] * 3 + [anywhere] * 12,
        out_specs=(anywhere, anywhere),
        out_shape=(
            jax.ShapeDtypeStruct(matrix.shape, F32),
            jax.ShapeDtypeStruct(right_sides.shape, F32),
        ),
        scratch_shapes=[
            pair(NB, EDGE),
            pair(NB, NB),
            pair(NB, width - NB),
            pair(NB, NB),
            pair(NB, width - NB),
        ]
        + [pltpu.SemaphoreType.DMA((2,))] * 5,
        compiler_params=pltpu.CompilerParams(vmem_limit_bytes=48 << 20),
        cost_estimate=pl.CostEstimate(flops=20_000_000_000, bytes_accessed=44 << 20, transcendentals=0),
        name="update",
    )(jnp.stack([row, col, z, y]), weights, special, answer, *gathered, matrix, right_sides)


def solution(mesh):
    specs = (P("row", "col"), P("row", None))
    return jax.shard_map(body, mesh=mesh, in_specs=specs, out_specs=specs, check_vma=False)
```

```python
import functools
import jax
import jax.numpy as jnp
from jax import lax
from jax.experimental import pallas as pl
from jax.experimental.pallas import tpu as pltpu
from jax.sharding import PartitionSpec as P

NB = 512
EDGE = 1024
TILE = 128
AXES = ("row", "col")
F32 = jnp.float32
BF16 = jnp.bfloat16
NN = (((1,), (0,)), ((), ()))
NT = (((1,), (1,)), ((), ()))
VMEM = pl.BlockSpec(memory_space=pltpu.VMEM)


def device_index(x, y, z, core):
    return ((x % 2) * 2 + core) * 32 + (z % 4) * 8 + (y % 4) * 2 + (x % 4) // 2


def route(rule):
    pairs = []
    for x in range(4):
        for y in range(4):
            for z in range(4):
                for core in range(2):
                    target = rule(x, y, z, core)
                    if target is not None:
                        pairs.append((device_index(x, y, z, core), device_index(*target)))
    return pairs


def send(value, rule):
    return lax.ppermute(value, AXES, route(rule))


def swap_cores(value):
    return send(value, lambda x, y, z, c: (x, y, z, 1 - c))


def split(value):
    high = value.astype(BF16)
    return high, (value - high.astype(F32)).astype(BF16)


def dot3(a, b, dims=NN):
    ah, al = split(a)
    bh, bl = split(b)
    mul = lambda p, q: lax.dot_general(p, q, dims, preferred_element_type=F32)
    return mul(ah, bh) + (mul(ah, bl) + mul(al, bh))


def dot_full(a, b, dims=NN):
    return lax.dot_general(a, b, dims, precision=lax.Precision.HIGHEST, preferred_element_type=F32)


def factor_tile(work, inverse, factor_t):
    rows = lax.broadcasted_iota(jnp.int32, (TILE, TILE), 0)
    lanes = lax.broadcasted_iota(jnp.int32, (TILE, TILE), 1)
    inverse[...] = jnp.where(rows == lanes, F32(1), F32(0))
    lane8 = lax.broadcasted_iota(jnp.int32, (8, TILE), 1)
    row8 = lax.broadcasted_iota(jnp.int32, (8, TILE), 0)
    spread = lambda v, s: jnp.broadcast_to(v[:, s : s + 1], (8, TILE))
    tile = lambda g: pl.ds(pl.multiple_of(g % 16 * 8, 8), 8)

    def pivot(g, top, cols, eye, below, below_eye):
        whole = lambda v, t: jnp.broadcast_to(v[t : t + 1, :], (8, TILE))
        e = [[whole(cols[s], t) if s <= t else None for s in range(8)] for t in range(8)]
        low = [[None] * 8 for _ in range(8)]
        scale = [None] * 8
        for s in range(8):
            scale[s] = r = lax.rsqrt(e[s][s])
            for t in range(s + 1, 8):
                low[t][s] = e[t][s] * r
            for u in range(s + 1, 8):
                for t in range(u, 8):
                    e[t][u] = e[t][u] - low[t][s] * low[u][s]
        inv = [[None] * 8 for _ in range(8)]
        for s in range(8):
            inv[s][s] = scale[s]
            for t in range(s + 1, 8):
                total = low[t][s] * inv[s][s]
                for u in range(s + 1, t):
                    total = total + low[t][u] * inv[u][s]
                inv[t][s] = -total * scale[t]
        upper = None
        solved = None
        for t in range(8):
            column = jnp.where(row8 == t, inv[t][t], F32(0))
            for s in range(t + 1, 8):
                column = jnp.where(row8 == s, inv[s][t], column)
            a = column * top[t : t + 1, :]
            b = column * eye[t : t + 1, :]
            upper = a if upper is None else upper + a
            solved = b if solved is None else solved + b
        upper = jnp.where(lane8 < TILE - 8 * g, upper, F32(0))
        back = None
        for s in range(8):
            column = jnp.where(row8 == s, inv[s][s], F32(0))
            for t in range(s):
                column = jnp.where(row8 == t, inv[s][t], column)
            a = column * upper[s : s + 1, :]
            b = column * solved[s : s + 1, :]
            back = (a, b) if back is None else (back[0] + a, back[1] + b)
        below, below_eye = apply(below, below_eye, back)
        cols = tuple(spread(below, 8 + s) for s in range(8))
        return upper, solved, back, pltpu.roll(below, TILE - 8, 1), below_eye, cols

    def apply(new, row, back):
        mults = [spread(new, s) for s in range(8)]
        for s in range(8):
            new = new - mults[s] * back[0][s : s + 1, :]
            row = row - mults[s] * back[1][s : s + 1, :]
        return new, row

    def group(last, g, carry):
        back, top, eye, cols = carry
        below, below_eye = apply(work[16:24, :], inverse[tile(g + 2), :], back)
        for q in range(3, last):
            new, row = apply(work[8 * q : 8 * q + 8, :], inverse[tile(g + q), :], back)
            work[8 * q - 8 : 8 * q, :] = pltpu.roll(new, TILE - 8, 1)
            inverse[tile(g + q), :] = row
        work[8 * last - 8 : 8 * last, :] = jnp.zeros((8, TILE), F32)
        carry = pivot(g + 1, top, cols, eye, pltpu.roll(below, TILE - 8, 1), below_eye)
        factor_t[tile(g + 1), :] = pltpu.roll(carry[0], 8 * (g + 1), 1)
        inverse[tile(g + 1), :] = carry[1]
        return carry[2:]

    top = work[0:8, :]
    cols = tuple(spread(top, s) for s in range(8))
    carry = pivot(0, top, cols, inverse[0:8, :], work[8:16, :], inverse[8:16, :])
    factor_t[0:8, :] = carry[0]
    inverse[0:8, :] = carry[1]
    carry = carry[2:]
    for first, stop, last in ((0, 3, 16), (3, 6, 13), (6, 9, 10), (9, 12, 7), (12, 15, 4)):
        carry = lax.fori_loop(first, stop, functools.partial(group, last), carry)


def factor_blocks(blocks, mat, low, inv, inv_t, work, tile_inv, tile_t):
    rows = lax.broadcasted_iota(jnp.int32, (TILE, TILE), 0)
    lanes = lax.broadcasted_iota(jnp.int32, (TILE, TILE), 1)
    for b in blocks:
        s, e = b * TILE, (b + 1) * TILE
        work[...] = mat[s:e, s:e]
        factor_tile(work, tile_inv, tile_t)
        x = jnp.where(rows >= lanes, tile_inv[...], F32(0))
        low[s:e, s:e] = jnp.where(rows >= lanes, tile_t[...].T, F32(0))
        inv[s:e, s:e] = x
        inv_t[s:e, s:e] = x.T
        if b > 0:
            left = dot_full(low[s:e, 0:s], inv[0:s, 0:s])
            left = -dot_full(x, left)
            inv[s:e, 0:s] = left
            inv_t[0:s, s:e] = left.T
        if e < NB:
            panel = dot_full(mat[e:NB, s:e], x, NT)
            low[e:NB, s:e] = panel
            for c in range(e, NB, 2 * TILE):
                d = min(c + 2 * TILE, NB)
                mat[c:NB, c:d] = mat[c:NB, c:d] - dot_full(panel[c - e :], panel[c - e : d - e], NT)


def place_quarters(place, mine, other, target, core):
    quarter = NB // 4
    for d in range(4):
        at = pl.multiple_of((place[0] + d) % 4 * quarter, quarter)
        rows = slice(d * quarter, (d + 1) * quarter)
        target[pl.ds(at, quarter), :] = jnp.where(place[1] == core, mine[rows, :], other[rows, :])


def first_kernel(place, mine, other, mat, low, inv, inv_t, work, tile_inv, tile_t):
    place_quarters(place, mine, other, mat, 0)
    low[...] = jnp.zeros_like(low)
    inv[...] = jnp.zeros_like(inv)
    inv_t[...] = jnp.zeros_like(inv_t)
    factor_blocks((0,), mat, low, inv, inv_t, work, tile_inv, tile_t)


def middle_kernel(m, l, i, t, mat, low, inv, inv_t, *tiles):
    carry_on((1,), (m, l, i, t), mat, low, inv, inv_t, tiles)


def open_kernel(source, mat, low, inv, inv_t, work, tile_inv, tile_t):
    mat[...] = source[...]
    low[...] = jnp.zeros_like(low)
    inv[...] = jnp.zeros_like(inv)
    inv_t[...] = jnp.zeros_like(inv_t)
    factor_blocks((0, 1), mat, low, inv, inv_t, work, tile_inv, tile_t)


def carry_on(blocks, sources, mat, low, inv, inv_t, tiles):
    for source, target in zip(sources, (mat, low, inv, inv_t)):
        target[...] = source[...]
    factor_blocks(blocks, mat, low, inv, inv_t, *tiles)


def close_kernel(m, l, i, t, low, inv, inv_t, mat, *tiles):
    carry_on((2, 3), (m, l, i, t), mat, low, inv, inv_t, tiles)


def below_kernel(place, m, l, i, t, mine, other, edge, far_edge, low, inv, inv_t, below, below_t, rest, mat, *tiles):
    carry_on((2, 3), (m, l, i, t), mat, low, inv, inv_t, tiles)
    place_quarters(place, mine, other, rest, 1)
    panel = dot_full(rest[...], inv_t[...])
    below[...] = panel
    below_t[...] = panel.T
    place_quarters(place, edge, far_edge, rest, 1)
    rest[...] = rest[...] - dot_full(panel, panel, NT)


def squares(kernel, name, outs, held, *args, place=()):
    return pl.pallas_call(
        kernel,
        out_shape=(jax.ShapeDtypeStruct((NB, NB), F32),) * outs,
        in_specs=[pl.BlockSpec(memory_space=pltpu.SMEM)] * len(place) + [VMEM] * len(args),
        out_specs=(VMEM,) * outs,
        scratch_shapes=[pltpu.VMEM((NB, NB), F32)] * held + [pltpu.VMEM((TILE, TILE), F32)] * 3,
        compiler_params=pltpu.CompilerParams(vmem_limit_bytes=24 << 20),
        cost_estimate=pl.CostEstimate(flops=30_000_000_000, bytes_accessed=len(args) << 20, transcendentals=0),
        name=name,
    )(*place, *args)


def solve_kernel(col_ref, g0, g1, inv0, inv0_t, below, below_t, inv1, inv1_t, parts, y, mid):
    col = col_ref[0]

    def put(at, value):
        high, low = split(value)
        for k, part in enumerate((high, low, high)):
            parts[k * EDGE + at : k * EDGE + at + NB, :] = part

    half = NB // 2
    y0 = jnp.concatenate([dot3(inv0[0:half, 0:half], g0[0:half, :]), dot3(inv0[half:, :], g0[...])], axis=0)
    rest = g1[...] - dot3(below[...], y0)
    y1 = jnp.concatenate([dot3(inv1[0:half, 0:half], rest[0:half, :]), dot3(inv1[half:, :], rest)], axis=0)
    rows = lax.broadcasted_iota(jnp.int32, (NB, NB), 0)
    lanes = lax.broadcasted_iota(jnp.int32, (NB, NB), 1)
    y[0:NB, :] = y0[:, NB:]
    y[NB:, :] = y1[:, NB:]
    unit = jnp.where(rows == lanes, F32(-1), F32(0))
    mid[0:NB, NB:] = y0[:, NB:]
    mid[NB:, NB:] = y1[:, NB:]
    mid[0:NB, 0:NB] = jnp.where(col == 0, unit, jnp.where(col == 1, F32(0), y0[:, 0:NB]))
    mid[NB:, 0:NB] = jnp.where(col == 1, unit, jnp.where(col == 0, F32(0), y1[:, 0:NB]))
    w1 = jnp.concatenate(
        [dot3(inv1_t[0:half, :], mid[NB:, :]), dot3(inv1_t[half:, half:], mid[NB + half :, :])], axis=0
    )
    put(NB, w1)
    z0 = mid[0:NB, :] - dot3(below_t[...], w1)
    w0 = jnp.concatenate([dot3(inv0_t[0:half, :], z0), dot3(inv0_t[half:, half:], z0[half:, :])], axis=0)
    put(0, w0)


def update_kernel(place, weights, special, y, *refs):
    a_refs, b_refs = refs[0:5], refs[5:10]
    mat, rhs, out, out_rhs, rbuf, mbuf, vbuf, obuf, qbuf, rsem, msem, vsem, osem, qsem = refs[10:]
    row, col, here_z, here_y = place[0], place[1], place[2], place[3]
    steps = 8

    def chunk(s, k):
        z = (here_z + jnp.where(s < 4, s, k)) % 4
        v = (here_y + jnp.where(s < 4, k, s - 4)) % 4
        return pl.multiple_of((z * 4 + v) * 2 * TILE + jnp.where(s < 4, 0, TILE), TILE)

    def load(s, slot):
        for t in range(steps):
            refs5 = a_refs if t < 4 else b_refs
            own, plus, minus, far0, far1 = refs5

            @pl.when(s == t)
            def _(t=t, own=own, plus=plus, minus=minus, far0=far0, far1=far1):
                if t % 4 == 2:
                    pltpu.make_async_copy(far0, rbuf.at[slot, pl.ds(0, NB // 2)], rsem.at[slot]).start()
                    pltpu.make_async_copy(far1, rbuf.at[slot, pl.ds(NB // 2, NB // 2)], rsem.at[slot]).start()
                else:
                    pltpu.make_async_copy((own, plus, None, minus)[t % 4], rbuf.at[slot], rsem.at[slot]).start()

        for k in range(4):
            at = chunk(s, k)
            pltpu.make_async_copy(mat.at[pl.ds(at, TILE)], mbuf.at[slot, pl.ds(k * TILE, TILE)], msem.at[slot]).start()
            pltpu.make_async_copy(rhs.at[pl.ds(at, TILE)], vbuf.at[slot, pl.ds(k * TILE, TILE)], vsem.at[slot]).start()

    def drain(slot):
        pltpu.make_async_copy(obuf.at[slot], obuf.at[slot], osem.at[slot]).wait()
        pltpu.make_async_copy(qbuf.at[slot], qbuf.at[slot], qsem.at[slot]).wait()

    mul = lambda p, q: lax.dot_general(p, q, NN, preferred_element_type=F32)
    load(0, 0)

    def step(s, carry):
        slot = s % 2

        @pl.when(s + 1 < steps)
        def _():
            load(s + 1, 1 - slot)

        pltpu.make_async_copy(rbuf.at[slot], rbuf.at[slot], rsem.at[slot]).wait()
        pltpu.make_async_copy(mbuf.at[slot], mbuf.at[slot], msem.at[slot]).wait()
        pltpu.make_async_copy(vbuf.at[slot], vbuf.at[slot], vsem.at[slot]).wait()

        @pl.when(s >= 2)
        def _():
            drain(slot)

        rh, rl = split(rbuf[slot])
        acc = mul(jnp.concatenate([rh, rh, rl], axis=1), weights[...])
        obuf[slot] = jnp.where(col < 2, F32(0), mbuf[slot]) - acc[:, 0:NB]
        qbuf[slot] = vbuf[slot] - acc[:, NB:]
        for k in range(4):
            at = chunk(s, k)

            @pl.when(jnp.logical_and(row < 2, at < NB))
            def _():
                obuf[slot, pl.ds(k * TILE, TILE), :] = special[pl.ds(pl.multiple_of(at % NB, TILE), TILE), :]
                qbuf[slot, pl.ds(k * TILE, TILE), :] = y[pl.ds(pl.multiple_of(at % NB, TILE), TILE), :]

            pltpu.make_async_copy(obuf.at[slot, pl.ds(k * TILE, TILE)], out.at[pl.ds(at, TILE)], osem.at[slot]).start()
            pltpu.make_async_copy(
                qbuf.at[slot, pl.ds(k * TILE, TILE)], out_rhs.at[pl.ds(at, TILE)], qsem.at[slot]
            ).start()
        return carry

    lax.fori_loop(0, steps, step, 0)
    drain(0)
    drain(1)


def ordered(parts, first):
    return jnp.concatenate([lax.select_n(first, *(parts[(m - f) % 4] for f in range(4))) for m in range(4)], axis=0)


def join_kernel(*refs):
    parts, joined = refs[:8], refs[8:]
    for k in range(8):
        joined[k // 4][k % 4 * TILE : (k % 4 + 1) * TILE, :] = parts[k][...]


def join(*parts):
    return pl.pallas_call(
        join_kernel,
        out_shape=(jax.ShapeDtypeStruct((4 * TILE, EDGE), F32),) * 2,
        in_specs=[VMEM] * 8,
        out_specs=(VMEM,) * 2,
        compiler_params=pltpu.CompilerParams(vmem_limit_bytes=12 << 20),
        cost_estimate=pl.CostEstimate(flops=0, bytes_accessed=8 << 20, transcendentals=0),
        name="join",
    )(*parts)


def turn_kernel(source, target):
    target[...] = source[...].T


def turn(value):
    return pl.pallas_call(
        turn_kernel,
        out_shape=jax.ShapeDtypeStruct(value.shape, F32),
        in_specs=[VMEM],
        out_specs=VMEM,
        compiler_params=pltpu.CompilerParams(vmem_limit_bytes=8 << 20),
        cost_estimate=pl.CostEstimate(flops=0, bytes_accessed=2 << 20, transcendentals=0),
        name="turn",
    )(value)


def ring(axis, d):
    if axis == "y":
        return lambda X, Y, Z, C: (X, Y - d, Z, C)
    return lambda X, Y, Z, C: (X, Y, Z - d, C)


def tie(*values):
    return lax.optimization_barrier(values)


def body(matrix, right_sides):
    row = lax.axis_index("row")
    col = lax.axis_index("col")
    core, x_lo = row % 2, row // 2
    z, y, x = col // 8, col // 2 % 4, col % 2 * 2 + row // 2
    first = matrix[0:NB]

    part, half = NB // 4, NB // 2
    turned = turn(first)

    recv = []
    for d in (1, 2, 3):
        block = jnp.where(x == 2, (2 + d) % 4, d)
        recv.append(
            send(
                lax.dynamic_slice_in_dim(first, block * part, part, 0),
                lambda X, Y, Z, C, d=d: (X + d, Y, Z, C) if (Y, Z) == (0, 0) and X % 2 == 0 else None,
            )
        )
    here = lax.dynamic_slice_in_dim(first, x * part, part, 0)
    r1, r2, r3 = recv
    main = jnp.where(x == 0, here, jnp.where(x == 1, r1, jnp.where(x == 2, r2, r3)))
    corner = jnp.where(x == 0, r2, jnp.where(x == 1, r3, jnp.where(x == 2, here, r1)))
    held, turned = tie(jnp.concatenate([main, corner], axis=0), turned)

    def strew(m):
        def rule(X, Y, Z, C):
            if X % 2:
                return None
            u, v = m // 2 ^ C, m % 2 ^ C
            return (2 * (X // 2 ^ v) + Y % 2, Y // 2 * 2 + (Y % 2 ^ u), Z, X // 2)

        h = jnp.bitwise_xor(jnp.bitwise_xor(y % 2, m // 2), core)
        return send(lax.dynamic_slice_in_dim(turned, h * half, half, 0), rule)

    small = held.shape[0] // 4
    mine = jnp.where(z == 0, held[0:small], F32(0))
    for d in (1, 2, 3):
        mine = mine + send(
            held[d * small : (d + 1) * small], lambda X, Y, Z, C, d=d: (X, Y, d, C) if (Y, Z) == (0, 0) else None
        )
    got = [strew(0), strew(1)]
    mine, turned, *got = tie(mine, turned, *got)

    every = jnp.where(y == 0, mine, F32(0))
    for d in (1, 2, 3):
        every = every + send(mine, lambda X, Y, Z, C, d=d: (X, d, Z, C) if Y == 0 else None)
    got += [strew(2), strew(3)]
    (every,) = tie(every)

    zs = [every] + [send(every, ring("z", d)) for d in (1, 2, 3)]
    u = jnp.bitwise_xor(y % 2, x % 2)
    v = jnp.bitwise_xor(x // 2, core)
    pick = lambda a, b, p: jnp.where(a == 0, jnp.where(b == 0, p[0], p[1]), jnp.where(b == 0, p[2], p[3]))
    piece = jnp.concatenate([pick(u, v, got), pick(1 - u, 1 - v, got)], axis=1)
    piece_a, piece_b = piece[0:TILE], piece[TILE:]
    ring_z = ordered(zs, z)
    ring_z, piece_a, piece_b = tie(ring_z, piece_a, piece_b)

    mains = [ring_z[0:part]] + [send(ring_z[0:part], lambda X, Y, Z, C, d=d: (X - d, Y, Z, C)) for d in (1, 2, 3)]
    a1, a3 = send(piece_a, ring("y", 1)), send(piece_a, ring("y", 3))
    main = jnp.concatenate(mains, axis=0)
    main, a1, a3, piece_a, piece_b = tie(main, a1, a3, piece_a, piece_b)
    other_main = swap_cores(main)
    a2, b1 = send(piece_a, ring("y", 2)), send(piece_b, ring("z", 1))
    tail = ring_z[part:]
    main, other_main, tail = tie(main, other_main, tail)
    corners = [tail] + [send(tail, lambda X, Y, Z, C, d=d: (X - d, Y, Z, C)) for d in (1, 2, 3)]

    place = (jnp.stack([x, core]),)
    state = squares(first_kernel, "open0", 4, 0, main, other_main, place=place)

    state, a2, b1, piece_b = tie(state, a2, b1, piece_b)
    b2, b3 = send(piece_b, ring("z", 2)), send(piece_b, ring("z", 3))
    state = squares(middle_kernel, "middle0", 4, 0, *state)

    state, b2, b3, corners = tie(state, b2, b3, corners)
    corner = jnp.concatenate(corners, axis=0)
    other_corner = swap_cores(corner)
    rows_a, rows_b = join(piece_a, a1, a2, a3, piece_b, b1, b2, b3)
    fars = []
    for rows, axis in ((rows_a, "z"), (rows_b, "y")):
        fars.append((send(rows, ring(axis, 1)), send(rows, ring(axis, 3))))
    first_rows, top_rhs, other_corner = tie(first, right_sides[0:NB], other_corner)

    top = jnp.concatenate([first_rows, top_rhs], axis=1)
    crossed = send(top, lambda X, Y, Z, C: (X + 1, Y, Z, C) if X % 2 == 0 else None)
    l0, inv0, inv0_t, below, below_t, rest = squares(
        below_kernel, "below0", 6, 1, *state, main, other_main, corner, other_corner, place=place
    )
    state = squares(open_kernel, "open1", 4, 0, rest)

    state, fars, crossed = tie(state, fars, crossed)
    own = jnp.where(x_lo == 0, top, crossed)
    partner = swap_cores(own)
    gathered = []
    for (plus, minus), rows, axis in ((fars[0], rows_a, "z"), (fars[1], rows_b, "y")):
        far0 = send(plus[0:half], ring(axis, 1))
        far1 = send(minus[half:], ring(axis, 3))
        gathered += [rows, plus, minus, far0, far1]

    l1, inv1, inv1_t = squares(close_kernel, "close1", 3, 1, *state)
    g0 = jnp.where(core == 0, own, partner)
    g1 = jnp.where(core == 0, partner, own)

    width = NB + right_sides.shape[1]
    weights, answer = pl.pallas_call(
        solve_kernel,
        out_shape=(
            jax.ShapeDtypeStruct((3 * EDGE, width), BF16),
            jax.ShapeDtypeStruct((EDGE, width - NB), F32),
        ),
        in_specs=[pl.BlockSpec(memory_space=pltpu.SMEM)] + [VMEM] * 8,
        out_specs=(VMEM,) * 2,
        scratch_shapes=[pltpu.VMEM((EDGE, width), F32)],
        compiler_params=pltpu.CompilerParams(vmem_limit_bytes=48 << 20),
        cost_estimate=pl.CostEstimate(flops=10_000_000_000, bytes_accessed=16 << 20, transcendentals=0),
        name="solve",
    )(col.reshape(1), g0, g1, inv0, inv0_t, below, below_t, inv1, inv1_t)

    lower = jnp.where(row == 0, jnp.where(col == 0, l0, F32(0)), jnp.where(col == 0, below, l1))
    special = jnp.where(col < 2, lower, F32(0))
    answer = lax.dynamic_slice_in_dim(answer, row % 2 * NB, NB, 0)

    anywhere = pl.BlockSpec(memory_space=pl.ANY)
    pair = lambda *shape: pltpu.VMEM((2,) + shape, F32)
    return pl.pallas_call(
        update_kernel,
        in_specs=[pl.BlockSpec(memory_space=pltpu.SMEM)] + [VMEM] * 3 + [anywhere] * 12,
        out_specs=(anywhere, anywhere),
        out_shape=(
            jax.ShapeDtypeStruct(matrix.shape, F32),
            jax.ShapeDtypeStruct(right_sides.shape, F32),
        ),
        scratch_shapes=[
            pair(NB, EDGE),
            pair(NB, NB),
            pair(NB, width - NB),
            pair(NB, NB),
            pair(NB, width - NB),
        ]
        + [pltpu.SemaphoreType.DMA((2,))] * 5,
        compiler_params=pltpu.CompilerParams(vmem_limit_bytes=48 << 20),
        cost_estimate=pl.CostEstimate(flops=20_000_000_000, bytes_accessed=44 << 20, transcendentals=0),
        name="update",
    )(jnp.stack([row, col, z, y]), weights, special, answer, *gathered, matrix, right_sides)


def solution(mesh):
    specs = (P("row", "col"), P("row", None))
    return jax.shard_map(body, mesh=mesh, in_specs=specs, out_specs=specs, check_vma=False)
```

```python
import functools
import jax
import jax.numpy as jnp
from jax import lax
from jax.experimental import pallas as pl
from jax.experimental.pallas import tpu as pltpu
from jax.sharding import PartitionSpec as P

NB = 512
EDGE = 1024
TILE = 128
AXES = ("row", "col")
F32 = jnp.float32
BF16 = jnp.bfloat16
NN = (((1,), (0,)), ((), ()))
NT = (((1,), (1,)), ((), ()))
VMEM = pl.BlockSpec(memory_space=pltpu.VMEM)


def device_index(x, y, z, core):
    return ((x % 2) * 2 + core) * 32 + (z % 4) * 8 + (y % 4) * 2 + (x % 4) // 2


def route(rule):
    pairs = []
    for x in range(4):
        for y in range(4):
            for z in range(4):
                for core in range(2):
                    target = rule(x, y, z, core)
                    if target is not None:
                        pairs.append((device_index(x, y, z, core), device_index(*target)))
    return pairs


def send(value, rule):
    return lax.ppermute(value, AXES, route(rule))


def swap_cores(value):
    return send(value, lambda x, y, z, c: (x, y, z, 1 - c))


def split(value):
    high = value.astype(BF16)
    return high, (value - high.astype(F32)).astype(BF16)


def dot3(a, b, dims=NN):
    ah, al = split(a)
    bh, bl = split(b)
    mul = lambda p, q: lax.dot_general(p, q, dims, preferred_element_type=F32)
    return mul(ah, bh) + (mul(ah, bl) + mul(al, bh))


def dot_full(a, b, dims=NN):
    return lax.dot_general(a, b, dims, precision=lax.Precision.HIGHEST, preferred_element_type=F32)


def factor_tile(work, inverse, factor_t):
    rows = lax.broadcasted_iota(jnp.int32, (TILE, TILE), 0)
    lanes = lax.broadcasted_iota(jnp.int32, (TILE, TILE), 1)
    inverse[...] = jnp.where(rows == lanes, F32(1), F32(0))
    lane8 = lax.broadcasted_iota(jnp.int32, (8, TILE), 1)
    row8 = lax.broadcasted_iota(jnp.int32, (8, TILE), 0)
    spread = lambda v, s: jnp.broadcast_to(v[:, s : s + 1], (8, TILE))
    tile = lambda g: pl.ds(pl.multiple_of(g % 16 * 8, 8), 8)

    def pivot(g, top, cols, eye, below, below_eye):
        whole = lambda v, t: jnp.broadcast_to(v[t : t + 1, :], (8, TILE))
        e = [[whole(cols[s], t) if s <= t else None for s in range(8)] for t in range(8)]
        low = [[None] * 8 for _ in range(8)]
        scale = [None] * 8
        for s in range(8):
            scale[s] = r = lax.rsqrt(e[s][s])
            for t in range(s + 1, 8):
                low[t][s] = e[t][s] * r
            for u in range(s + 1, 8):
                for t in range(u, 8):
                    e[t][u] = e[t][u] - low[t][s] * low[u][s]
        inv = [[None] * 8 for _ in range(8)]
        for s in range(8):
            inv[s][s] = scale[s]
            for t in range(s + 1, 8):
                total = low[t][s] * inv[s][s]
                for u in range(s + 1, t):
                    total = total + low[t][u] * inv[u][s]
                inv[t][s] = -total * scale[t]
        upper = None
        solved = None
        for t in range(8):
            column = jnp.where(row8 == t, inv[t][t], F32(0))
            for s in range(t + 1, 8):
                column = jnp.where(row8 == s, inv[s][t], column)
            a = column * top[t : t + 1, :]
            b = column * eye[t : t + 1, :]
            upper = a if upper is None else upper + a
            solved = b if solved is None else solved + b
        upper = jnp.where(lane8 < TILE - 8 * g, upper, F32(0))
        back = None
        for s in range(8):
            column = jnp.where(row8 == s, inv[s][s], F32(0))
            for t in range(s):
                column = jnp.where(row8 == t, inv[s][t], column)
            a = column * upper[s : s + 1, :]
            b = column * solved[s : s + 1, :]
            back = (a, b) if back is None else (back[0] + a, back[1] + b)
        below, below_eye = apply(below, below_eye, back)
        cols = tuple(spread(below, 8 + s) for s in range(8))
        return upper, solved, back, pltpu.roll(below, TILE - 8, 1), below_eye, cols

    def apply(new, row, back):
        mults = [spread(new, s) for s in range(8)]
        for s in range(8):
            new = new - mults[s] * back[0][s : s + 1, :]
            row = row - mults[s] * back[1][s : s + 1, :]
        return new, row

    def group(last, g, carry):
        back, top, eye, cols = carry
        below, below_eye = apply(work[16:24, :], inverse[tile(g + 2), :], back)
        for q in range(3, last):
            new, row = apply(work[8 * q : 8 * q + 8, :], inverse[tile(g + q), :], back)
            work[8 * q - 8 : 8 * q, :] = pltpu.roll(new, TILE - 8, 1)
            inverse[tile(g + q), :] = row
        work[8 * last - 8 : 8 * last, :] = jnp.zeros((8, TILE), F32)
        carry = pivot(g + 1, top, cols, eye, pltpu.roll(below, TILE - 8, 1), below_eye)
        factor_t[tile(g + 1), :] = pltpu.roll(carry[0], 8 * (g + 1), 1)
        inverse[tile(g + 1), :] = carry[1]
        return carry[2:]

    top = work[0:8, :]
    cols = tuple(spread(top, s) for s in range(8))
    carry = pivot(0, top, cols, inverse[0:8, :], work[8:16, :], inverse[8:16, :])
    factor_t[0:8, :] = carry[0]
    inverse[0:8, :] = carry[1]
    carry = carry[2:]
    for first, stop, last in ((0, 3, 16), (3, 6, 13), (6, 9, 10), (9, 12, 7), (12, 15, 4)):
        carry = lax.fori_loop(first, stop, functools.partial(group, last), carry)


def factor_blocks(blocks, mat, low, inv, inv_t, work, tile_inv, tile_t):
    rows = lax.broadcasted_iota(jnp.int32, (TILE, TILE), 0)
    lanes = lax.broadcasted_iota(jnp.int32, (TILE, TILE), 1)
    for b in blocks:
        s, e = b * TILE, (b + 1) * TILE
        work[...] = mat[s:e, s:e]
        factor_tile(work, tile_inv, tile_t)
        x = jnp.where(rows >= lanes, tile_inv[...], F32(0))
        low[s:e, s:e] = jnp.where(rows >= lanes, tile_t[...].T, F32(0))
        inv[s:e, s:e] = x
        inv_t[s:e, s:e] = x.T
        if b > 0:
            left = dot_full(low[s:e, 0:s], inv[0:s, 0:s])
            left = -dot_full(x, left)
            inv[s:e, 0:s] = left
            inv_t[0:s, s:e] = left.T
        if e < NB:
            panel = dot_full(mat[e:NB, s:e], x, NT)
            low[e:NB, s:e] = panel
            for c in range(e, NB, 2 * TILE):
                d = min(c + 2 * TILE, NB)
                mat[c:NB, c:d] = mat[c:NB, c:d] - dot_full(panel[c - e :], panel[c - e : d - e], NT)


def place_quarters(place, mine, other, target, core):
    quarter = NB // 4
    for d in range(4):
        at = pl.multiple_of((place[0] + d) % 4 * quarter, quarter)
        rows = slice(d * quarter, (d + 1) * quarter)
        target[pl.ds(at, quarter), :] = jnp.where(place[1] == core, mine[rows, :], other[rows, :])


def first_kernel(place, mine, other, mat, low, inv, inv_t, work, tile_inv, tile_t):
    place_quarters(place, mine, other, mat, 0)
    low[...] = jnp.zeros_like(low)
    inv[...] = jnp.zeros_like(inv)
    inv_t[...] = jnp.zeros_like(inv_t)
    factor_blocks((0, 1), mat, low, inv, inv_t, work, tile_inv, tile_t)


def open_kernel(source, mat, low, inv, inv_t, work, tile_inv, tile_t):
    mat[...] = source[...]
    low[...] = jnp.zeros_like(low)
    inv[...] = jnp.zeros_like(inv)
    inv_t[...] = jnp.zeros_like(inv_t)
    factor_blocks((0, 1), mat, low, inv, inv_t, work, tile_inv, tile_t)


def carry_on(sources, mat, low, inv, inv_t, tiles):
    for source, target in zip(sources, (mat, low, inv, inv_t)):
        target[...] = source[...]
    factor_blocks((2, 3), mat, low, inv, inv_t, *tiles)


def close_kernel(m, l, i, t, low, inv, inv_t, mat, *tiles):
    carry_on((m, l, i, t), mat, low, inv, inv_t, tiles)


def below_kernel(place, m, l, i, t, mine, other, edge, far_edge, low, inv, inv_t, below, below_t, rest, mat, *tiles):
    carry_on((m, l, i, t), mat, low, inv, inv_t, tiles)
    place_quarters(place, mine, other, rest, 1)
    panel = dot_full(rest[...], inv_t[...])
    below[...] = panel
    below_t[...] = panel.T
    place_quarters(place, edge, far_edge, rest, 1)
    rest[...] = rest[...] - dot_full(panel, panel, NT)


def squares(kernel, name, outs, held, *args, place=()):
    return pl.pallas_call(
        kernel,
        out_shape=(jax.ShapeDtypeStruct((NB, NB), F32),) * outs,
        in_specs=[pl.BlockSpec(memory_space=pltpu.SMEM)] * len(place) + [VMEM] * len(args),
        out_specs=(VMEM,) * outs,
        scratch_shapes=[pltpu.VMEM((NB, NB), F32)] * held + [pltpu.VMEM((TILE, TILE), F32)] * 3,
        compiler_params=pltpu.CompilerParams(vmem_limit_bytes=24 << 20),
        cost_estimate=pl.CostEstimate(flops=30_000_000_000, bytes_accessed=len(args) << 20, transcendentals=0),
        name=name,
    )(*place, *args)


def solve_kernel(col_ref, g0, g1, inv0, inv0_t, below, below_t, inv1, inv1_t, parts, y, mid):
    col = col_ref[0]

    def put(at, value):
        high, low = split(value)
        for k, part in enumerate((high, low, high)):
            parts[k * EDGE + at : k * EDGE + at + NB, :] = part

    half = NB // 2
    y0 = jnp.concatenate([dot3(inv0[0:half, 0:half], g0[0:half, :]), dot3(inv0[half:, :], g0[...])], axis=0)
    rest = g1[...] - dot3(below[...], y0)
    y1 = jnp.concatenate([dot3(inv1[0:half, 0:half], rest[0:half, :]), dot3(inv1[half:, :], rest)], axis=0)
    rows = lax.broadcasted_iota(jnp.int32, (NB, NB), 0)
    lanes = lax.broadcasted_iota(jnp.int32, (NB, NB), 1)
    y[0:NB, :] = y0[:, NB:]
    y[NB:, :] = y1[:, NB:]
    unit = jnp.where(rows == lanes, F32(-1), F32(0))
    mid[0:NB, NB:] = y0[:, NB:]
    mid[NB:, NB:] = y1[:, NB:]
    mid[0:NB, 0:NB] = jnp.where(col == 0, unit, jnp.where(col == 1, F32(0), y0[:, 0:NB]))
    mid[NB:, 0:NB] = jnp.where(col == 1, unit, jnp.where(col == 0, F32(0), y1[:, 0:NB]))
    w1 = jnp.concatenate(
        [dot3(inv1_t[0:half, :], mid[NB:, :]), dot3(inv1_t[half:, half:], mid[NB + half :, :])], axis=0
    )
    put(NB, w1)
    z0 = mid[0:NB, :] - dot3(below_t[...], w1)
    w0 = jnp.concatenate([dot3(inv0_t[0:half, :], z0), dot3(inv0_t[half:, half:], z0[half:, :])], axis=0)
    put(0, w0)


def update_kernel(place, weights, special, y, *refs):
    a_refs, b_refs = refs[0:5], refs[5:10]
    mat, rhs, out, out_rhs, rbuf, mbuf, vbuf, obuf, qbuf, rsem, msem, vsem, osem, qsem = refs[10:]
    row, col, here_z, here_y = place[0], place[1], place[2], place[3]
    steps = 8

    def chunk(s, k):
        z = (here_z + jnp.where(s < 4, s, k)) % 4
        v = (here_y + jnp.where(s < 4, k, s - 4)) % 4
        return pl.multiple_of((z * 4 + v) * 2 * TILE + jnp.where(s < 4, 0, TILE), TILE)

    def load(s, slot):
        for t in range(steps):
            refs5 = a_refs if t < 4 else b_refs
            own, plus, minus, far0, far1 = refs5

            @pl.when(s == t)
            def _(t=t, own=own, plus=plus, minus=minus, far0=far0, far1=far1):
                if t % 4 == 2:
                    pltpu.make_async_copy(far0, rbuf.at[slot, pl.ds(0, NB // 2)], rsem.at[slot]).start()
                    pltpu.make_async_copy(far1, rbuf.at[slot, pl.ds(NB // 2, NB // 2)], rsem.at[slot]).start()
                else:
                    pltpu.make_async_copy((own, plus, None, minus)[t % 4], rbuf.at[slot], rsem.at[slot]).start()

        for k in range(4):
            at = chunk(s, k)
            pltpu.make_async_copy(mat.at[pl.ds(at, TILE)], mbuf.at[slot, pl.ds(k * TILE, TILE)], msem.at[slot]).start()
            pltpu.make_async_copy(rhs.at[pl.ds(at, TILE)], vbuf.at[slot, pl.ds(k * TILE, TILE)], vsem.at[slot]).start()

    def drain(slot):
        pltpu.make_async_copy(obuf.at[slot], obuf.at[slot], osem.at[slot]).wait()
        pltpu.make_async_copy(qbuf.at[slot], qbuf.at[slot], qsem.at[slot]).wait()

    mul = lambda p, q: lax.dot_general(p, q, NN, preferred_element_type=F32)
    load(0, 0)

    def step(s, carry):
        slot = s % 2

        @pl.when(s + 1 < steps)
        def _():
            load(s + 1, 1 - slot)

        pltpu.make_async_copy(rbuf.at[slot], rbuf.at[slot], rsem.at[slot]).wait()
        pltpu.make_async_copy(mbuf.at[slot], mbuf.at[slot], msem.at[slot]).wait()
        pltpu.make_async_copy(vbuf.at[slot], vbuf.at[slot], vsem.at[slot]).wait()

        @pl.when(s >= 2)
        def _():
            drain(slot)

        rh, rl = split(rbuf[slot])
        acc = mul(jnp.concatenate([rh, rh, rl], axis=1), weights[...])
        obuf[slot] = jnp.where(col < 2, F32(0), mbuf[slot]) - acc[:, 0:NB]
        qbuf[slot] = vbuf[slot] - acc[:, NB:]
        for k in range(4):
            at = chunk(s, k)

            @pl.when(jnp.logical_and(row < 2, at < NB))
            def _():
                obuf[slot, pl.ds(k * TILE, TILE), :] = special[pl.ds(pl.multiple_of(at % NB, TILE), TILE), :]
                qbuf[slot, pl.ds(k * TILE, TILE), :] = y[pl.ds(pl.multiple_of(at % NB, TILE), TILE), :]

            pltpu.make_async_copy(obuf.at[slot, pl.ds(k * TILE, TILE)], out.at[pl.ds(at, TILE)], osem.at[slot]).start()
            pltpu.make_async_copy(
                qbuf.at[slot, pl.ds(k * TILE, TILE)], out_rhs.at[pl.ds(at, TILE)], qsem.at[slot]
            ).start()
        return carry

    lax.fori_loop(0, steps, step, 0)
    drain(0)
    drain(1)


def ordered(parts, first):
    return jnp.concatenate([lax.select_n(first, *(parts[(m - f) % 4] for f in range(4))) for m in range(4)], axis=0)


def turn_kernel(source, target):
    target[...] = source[...].T


def turn(value):
    return pl.pallas_call(
        turn_kernel,
        out_shape=jax.ShapeDtypeStruct(value.shape, F32),
        in_specs=[VMEM],
        out_specs=VMEM,
        compiler_params=pltpu.CompilerParams(vmem_limit_bytes=8 << 20),
        cost_estimate=pl.CostEstimate(flops=0, bytes_accessed=2 << 20, transcendentals=0),
        name="turn",
    )(value)


def ring(axis, d):
    if axis == "y":
        return lambda X, Y, Z, C: (X, Y - d, Z, C)
    return lambda X, Y, Z, C: (X, Y, Z - d, C)


def tie(*values):
    return lax.optimization_barrier(values)


def body(matrix, right_sides):
    row = lax.axis_index("row")
    col = lax.axis_index("col")
    core, x_lo = row % 2, row // 2
    z, y, x = col // 8, col // 2 % 4, col % 2 * 2 + row // 2
    first = matrix[0:NB]

    part, half = NB // 4, NB // 2
    turned = turn(first)

    recv = []
    for d in (1, 2, 3):
        block = jnp.where(x == 2, (2 + d) % 4, d)
        recv.append(
            send(
                lax.dynamic_slice_in_dim(first, block * part, part, 0),
                lambda X, Y, Z, C, d=d: (X + d, Y, Z, C) if (Y, Z) == (0, 0) and X % 2 == 0 else None,
            )
        )
    here = lax.dynamic_slice_in_dim(first, x * part, part, 0)
    r1, r2, r3 = recv
    main = jnp.where(x == 0, here, jnp.where(x == 1, r1, jnp.where(x == 2, r2, r3)))
    corner = jnp.where(x == 0, r2, jnp.where(x == 1, r3, jnp.where(x == 2, here, r1)))
    held, turned = tie(jnp.concatenate([main, corner], axis=0), turned)

    def strew(m):
        def rule(X, Y, Z, C):
            if X % 2:
                return None
            u, v = m // 2 ^ C, m % 2 ^ C
            return (2 * (X // 2 ^ v) + Y % 2, Y // 2 * 2 + (Y % 2 ^ u), Z, X // 2)

        h = jnp.bitwise_xor(jnp.bitwise_xor(y % 2, m // 2), core)
        return send(lax.dynamic_slice_in_dim(turned, h * half, half, 0), rule)

    small = held.shape[0] // 4
    mine = jnp.where(z == 0, held[0:small], F32(0))
    for d in (1, 2, 3):
        mine = mine + send(
            held[d * small : (d + 1) * small], lambda X, Y, Z, C, d=d: (X, Y, d, C) if (Y, Z) == (0, 0) else None
        )
    got = [strew(0), strew(1)]
    mine, turned, *got = tie(mine, turned, *got)

    every = jnp.where(y == 0, mine, F32(0))
    for d in (1, 2, 3):
        every = every + send(mine, lambda X, Y, Z, C, d=d: (X, d, Z, C) if Y == 0 else None)
    got += [strew(2), strew(3)]
    (every,) = tie(every)

    zs = [every] + [send(every, ring("z", d)) for d in (1, 2, 3)]
    u = jnp.bitwise_xor(y % 2, x % 2)
    v = jnp.bitwise_xor(x // 2, core)
    pick = lambda a, b, p: jnp.where(a == 0, jnp.where(b == 0, p[0], p[1]), jnp.where(b == 0, p[2], p[3]))
    piece = jnp.concatenate([pick(u, v, got), pick(1 - u, 1 - v, got)], axis=1)
    piece_a, piece_b = piece[0:TILE], piece[TILE:]
    ring_z = ordered(zs, z)
    ring_z, piece_a, piece_b = tie(ring_z, piece_a, piece_b)

    mains = [ring_z[0:part]] + [send(ring_z[0:part], lambda X, Y, Z, C, d=d: (X - d, Y, Z, C)) for d in (1, 2, 3)]
    a1, a3 = send(piece_a, ring("y", 1)), send(piece_a, ring("y", 3))
    main = jnp.concatenate(mains, axis=0)
    main, a1, a3, piece_a, piece_b = tie(main, a1, a3, piece_a, piece_b)
    other_main = swap_cores(main)
    a2, b1 = send(piece_a, ring("y", 2)), send(piece_b, ring("z", 1))
    tail = ring_z[part:]
    main, other_main, tail, a2, b1, piece_b = tie(main, other_main, tail, a2, b1, piece_b)
    corners = [tail] + [send(tail, lambda X, Y, Z, C, d=d: (X - d, Y, Z, C)) for d in (1, 2, 3)]
    b2, b3 = send(piece_b, ring("z", 2)), send(piece_b, ring("z", 3))

    place = (jnp.stack([x, core]),)
    state = squares(first_kernel, "open0", 4, 0, main, other_main, place=place)

    state, b2, b3, corners = tie(state, b2, b3, corners)
    corner = jnp.concatenate(corners, axis=0)
    other_corner = swap_cores(corner)
    rows_a = jnp.concatenate([piece_a, a1, a2, a3], axis=0)
    rows_b = jnp.concatenate([piece_b, b1, b2, b3], axis=0)
    fars = []
    for rows, axis in ((rows_a, "z"), (rows_b, "y")):
        fars.append((send(rows, ring(axis, 1)), send(rows, ring(axis, 3))))
    first_rows, top_rhs, other_corner = tie(first, right_sides[0:NB], other_corner)

    top = jnp.concatenate([first_rows, top_rhs], axis=1)
    crossed = send(top, lambda X, Y, Z, C: (X + 1, Y, Z, C) if X % 2 == 0 else None)
    l0, inv0, inv0_t, below, below_t, rest = squares(
        below_kernel, "below0", 6, 1, *state, main, other_main, corner, other_corner, place=place
    )
    state = squares(open_kernel, "open1", 4, 0, rest)

    state, fars, crossed = tie(state, fars, crossed)
    own = jnp.where(x_lo == 0, top, crossed)
    partner = swap_cores(own)
    gathered = []
    for (plus, minus), rows, axis in ((fars[0], rows_a, "z"), (fars[1], rows_b, "y")):
        far0 = send(plus[0:half], ring(axis, 1))
        far1 = send(minus[half:], ring(axis, 3))
        gathered += [rows, plus, minus, far0, far1]

    l1, inv1, inv1_t = squares(close_kernel, "close1", 3, 1, *state)
    g0 = jnp.where(core == 0, own, partner)
    g1 = jnp.where(core == 0, partner, own)

    width = NB + right_sides.shape[1]
    weights, answer = pl.pallas_call(
        solve_kernel,
        out_shape=(
            jax.ShapeDtypeStruct((3 * EDGE, width), BF16),
            jax.ShapeDtypeStruct((EDGE, width - NB), F32),
        ),
        in_specs=[pl.BlockSpec(memory_space=pltpu.SMEM)] + [VMEM] * 8,
        out_specs=(VMEM,) * 2,
        scratch_shapes=[pltpu.VMEM((EDGE, width), F32)],
        compiler_params=pltpu.CompilerParams(vmem_limit_bytes=48 << 20),
        cost_estimate=pl.CostEstimate(flops=10_000_000_000, bytes_accessed=16 << 20, transcendentals=0),
        name="solve",
    )(col.reshape(1), g0, g1, inv0, inv0_t, below, below_t, inv1, inv1_t)

    lower = jnp.where(row == 0, jnp.where(col == 0, l0, F32(0)), jnp.where(col == 0, below, l1))
    special = jnp.where(col < 2, lower, F32(0))
    answer = lax.dynamic_slice_in_dim(answer, row % 2 * NB, NB, 0)

    anywhere = pl.BlockSpec(memory_space=pl.ANY)
    pair = lambda *shape: pltpu.VMEM((2,) + shape, F32)
    return pl.pallas_call(
        update_kernel,
        in_specs=[pl.BlockSpec(memory_space=pltpu.SMEM)] + [VMEM] * 3 + [anywhere] * 12,
        out_specs=(anywhere, anywhere),
        out_shape=(
            jax.ShapeDtypeStruct(matrix.shape, F32),
            jax.ShapeDtypeStruct(right_sides.shape, F32),
        ),
        scratch_shapes=[
            pair(NB, EDGE),
            pair(NB, NB),
            pair(NB, width - NB),
            pair(NB, NB),
            pair(NB, width - NB),
        ]
        + [pltpu.SemaphoreType.DMA((2,))] * 5,
        compiler_params=pltpu.CompilerParams(vmem_limit_bytes=48 << 20),
        cost_estimate=pl.CostEstimate(flops=20_000_000_000, bytes_accessed=44 << 20, transcendentals=0),
        name="update",
    )(jnp.stack([row, col, z, y]), weights, special, answer, *gathered, matrix, right_sides)


def solution(mesh):
    specs = (P("row", "col"), P("row", None))
    return jax.shard_map(body, mesh=mesh, in_specs=specs, out_specs=specs, check_vma=False)
```
